32 devices in a mesh: section: 2 (over x), ep: 8 (over z, y), tp: 2 (over core).
Axes of the slice: x: 2, y: 2, z: 4, core: 2. Of those that a mesh axis runs over, the one named last changes fastest.
Arguments:
- section_rows: bfloat16 [2, 32, 7168], P('section', 'ep', 'tp'), may hold values from -6 to 6
- routes: int32 [2, 32, 2], P('section', 'ep'), may hold values from 0 to 3, all different within a row; in each aligned block of 4 rows (0 to 3, 4 to 7, ..., all dimensions but the last counted through in order) at most 3 rows name the same one
- route_weights: float32 [2, 32, 2], P('section', 'ep'), may hold values from 0.1 to 0.5
- in_gain: bfloat16 [2, 7168], P('section', 'tp'), may hold values from 0.099609375 to 1.8984375
- gate_up: bfloat16 [2, 8, 7168, 2048], P('section', 'ep', 'tp'), may hold values from -0.0625 to 0.0625
- down: bfloat16 [2, 8, 1024, 7168], P('section', 'ep', None, 'tp'), may hold values from -0.125 to 0.125
- out_gain: bfloat16 [2, 7168], P('section', 'tp'), may hold values from 0.099609375 to 1.8984375
Outputs:
- layer_out: bfloat16 [2, 32, 7168], P('section', 'ep', 'tp')
- handed: bfloat16 [2, 32, 7168], P('section', 'ep', 'tp')
The draws below stay inside these ranges and needn't reach their ends.
Inputs may be any that keep to these rules, and one draw needn't show every extreme that they name: `routes`: each row names 2 different experts. Among the 4 rows of one index of ep (aligned blocks of rows, both groups counted in order), no expert is named by more than 3 rows, a bound that some block reaches.
All inputs are finite; a program needn't handle non-finite values.
Results may differ from the reference program's by a relative error of at most 0.012.
Values may be sent and summed in bfloat16 or wider, within the bound.
A program may use at most 64 MiB of HBM per device.

```python
import math
import jax
import jax.numpy as jnp
import numpy as np
from jax import lax

D = 7168
HB = 2048
EXP_SPAN = 2
ROWS_DEV = 4
HPART = 1024
EXPERTS = 4
TOPK = 2
ROWS = 32
MOST = 3
N_EP = 8


def levels(key, dims, shards, least, top_value):
    loudness, own = 1.0, jax.random.fold_in(key, 6)
    for axis_at, blocks in shards:
        steps = jnp.exp(jax.random.uniform(jax.random.fold_in(own, axis_at), (blocks,), jnp.float32, least / len(shards), top_value / len(shards)))
        loudness = loudness * jnp.repeat(steps, dims[axis_at] // blocks).reshape([-1 if axis == axis_at else 1 for axis in range(len(dims))])
    return loudness


def assign_block(rng, own, number, rows, count, top, limit, slope):
    order = jax.random.permutation(rng, count)
    heavy_load, ordinary = load_shares(count, rows * top, limit, slope, True), load_shares(count, rows * top, limit, slope, False)
    places = jnp.arange(count)

    def named(tallies, offset_by):
        used = int((tallies > 0).sum())
        fixed = max(1, used // 4)
        moved = fixed + (places - fixed + offset_by * (used - fixed)) % max(1, count - fixed)
        return jnp.zeros((count,), jnp.int32).at[order[jnp.where(places < fixed, places, moved)]].set(jnp.asarray(tallies, jnp.int32))

    tallies = jnp.where(number % 4 == 0, named(heavy_load, number // 4), named(ordinary, number - number // 4 - 1))
    mixed = jax.random.permutation(jax.random.fold_in(own, 3), count)
    donor, sink = mixed[0:count // 2 * 2:2], mixed[1:count // 2 * 2:2]
    margin = jnp.minimum(tallies[donor] - 1, limit - tallies[sink]) // 2
    margin = jnp.where((donor == order[0]) | (sink == order[0]) | (tallies[sink] == 0), 0, jnp.maximum(margin, 0))
    moved = jax.random.randint(jax.random.fold_in(own, 4), (count // 2,), 0, 1 << 20) % (margin + 1)
    tallies = tallies.at[donor].add(-moved).at[sink].add(moved)
    items = jnp.searchsorted(jnp.cumsum(tallies), jnp.arange(rows * top), side="right").astype(jnp.int32)
    table = items.reshape(top, rows).T
    table = table[jax.random.permutation(jax.random.fold_in(own, 1), rows)]
    offset_by = jax.random.randint(jax.random.fold_in(own, 2), (rows, 1), 0, top)
    return jnp.take_along_axis(table, (jnp.arange(top)[None, :] + offset_by) % top, axis=1)


def load_shares(count, total, most, skew, full):
    portions = [(1 << 20) // math.isqrt(grade ** skew) + 1 for grade in range(1, count + 1)]
    largest = most if full else min(most, max(-(-total // count), total * portions[0] // sum(portions)))
    least = 1 if total - largest >= count - 1 else 0
    given, spare = [largest] + [least] * (count - 1), total - largest - least * (count - 1)
    while spare > 0:
        movable = [i for i in range(1, count) if given[i] < largest] or [i for i in range(1, count) if given[i] < most]
        pool, budget = sum([portions[i] for i in movable]), spare
        for i in movable:
            extra = min(most - given[i], max(1, budget * portions[i] // pool), spare)
            given[i] = given[i] + extra
            spare = spare - extra
    return np.array(given)


def scatter_about(stream_key, extent, spread, bound, pieces=(), kind=jnp.bfloat16):
    level = levels(stream_key, extent, pieces, -0.22, 0.18) if pieces else 1.0
    values = jax.random.normal(stream_key, extent, jnp.float32) * spread * level
    return jnp.minimum(jnp.maximum(values, -bound), bound).astype(kind)


def setup_inputs(seed: int = 0) -> dict:
    key_list = jax.random.split(jax.random.key(seed), 8)
    section_rows = scatter_about(key_list[0], (2, ROWS, D), 1.0, 6.0, ((0, 2), (1, 8), (2, 2)))
    routes_keys = jax.random.split(jax.random.fold_in(key_list[1], 1), 2 * ROWS // ROWS_DEV)
    routes_turns = jax.random.permutation(jax.random.fold_in(key_list[1], 3), 2 * ROWS // ROWS_DEV)
    routes = jax.vmap(lambda own, number: assign_block(jax.random.fold_in(key_list[1], 2), own, number, ROWS_DEV, EXPERTS, TOPK, MOST, 2))(routes_keys, routes_turns).reshape((2, ROWS, TOPK))
    route_weights = jnp.clip(0.1 + 0.4 * jax.random.uniform(key_list[2], (2, ROWS, TOPK), jnp.float32) ** levels(key_list[2], (2, ROWS, TOPK), ((0, 2), (1, 8)), -0.2, 0.2), 0.1, 0.5)
    in_gain = jnp.clip(1.0 + 0.18 * jax.random.normal(key_list[3], (2, D), jnp.float32), 0.099609375, 1.8984375).astype(jnp.bfloat16)
    gate_up = scatter_about(key_list[4], (2, EXPERTS * EXP_SPAN, D, 2 * HPART), D ** -0.5, 0.0625, ((0, 2), (1, 8), (2, 2)))
    down = scatter_about(key_list[5], (2, EXPERTS * EXP_SPAN, HPART, D), HB ** -0.5, 0.125, ((0, 2), (1, 8), (3, 2)))
    out_gain = jnp.clip(1.0 + 0.18 * jax.random.normal(key_list[6], (2, D), jnp.float32), 0.099609375, 1.8984375).astype(jnp.bfloat16)
    return dict(section_rows=section_rows, routes=routes, route_weights=route_weights, in_gain=in_gain, gate_up=gate_up, down=down, out_gain=out_gain)


def rms_scale(values):
    return lax.rsqrt(lax.optimization_barrier(jnp.mean(values * values, axis=1)) + 1e-06)

def moe_layer(inputs, route_ids, weights, gain, gate_proj, down_proj):
    values = inputs.astype(jnp.float32)
    normed = (values * rms_scale(values)[:, None] * gain.astype(jnp.float32)[None, :]).astype(jnp.bfloat16)
    blocks = route_ids.reshape(N_EP, ROWS_DEV * TOPK)
    expert_ids = jnp.arange(EXPERTS, dtype=jnp.int32)

    def ranks(block):
        onehot = (block[:, None] == expert_ids[None, :]).astype(jnp.int32)
        return lax.optimization_barrier(jnp.sum((jnp.cumsum(onehot, axis=0) - 1) * onehot, axis=1)).astype(jnp.int32)
    slot_rank = lax.map(ranks, blocks)
    source = jnp.arange(N_EP, dtype=jnp.int32)[:, None]
    row_index = source * ROWS_DEV + jnp.arange(ROWS_DEV * TOPK, dtype=jnp.int32)[None, :] // TOPK
    slot_ids = ((blocks * N_EP + source) * MOST + slot_rank).reshape(-1)
    span = N_EP * MOST
    row_of = jnp.full((EXPERTS * span,), ROWS, jnp.int32).at[slot_ids].set(row_index.reshape(-1))
    weight_of = jnp.zeros((EXPERTS * span,), jnp.float32).at[slot_ids].set(weights.reshape(-1).astype(jnp.float32))
    padded = jnp.concatenate([normed, jnp.zeros((1, D), jnp.bfloat16)], axis=0)
    gate_all = gate_proj.reshape(EXPERTS, EXP_SPAN, D, 2 * HPART)
    down_all = down_proj.reshape(EXPERTS, EXP_SPAN, HPART, D)

    def expert_step(total, expert):
        index = lax.dynamic_slice_in_dim(row_of, expert * span, span)
        scales = lax.dynamic_slice_in_dim(weight_of, expert * span, span)
        gathered = padded[index]
        gate_here = gate_all[expert]
        down_here = down_all[expert]
        summed = jnp.zeros((span, D), jnp.float32)
        for block in range(EXP_SPAN):
            both = jnp.dot(gathered, gate_here[block], preferred_element_type=jnp.float32)
            hidden = (jax.nn.silu(both[:, :HPART]) * both[:, HPART:]).astype(jnp.bfloat16)
            part = jnp.dot(hidden, down_here[block], preferred_element_type=jnp.float32).astype(jnp.bfloat16)
            summed = summed + part.astype(jnp.float32)
        total = total.at[index].add(summed * scales[:, None])
        return (total, None)
    start = jnp.zeros((ROWS + 1, D), jnp.float32)
    total, unused = lax.scan(expert_step, start, jnp.arange(EXPERTS, dtype=jnp.int32))
    return (values + total[:ROWS]).astype(jnp.bfloat16)

def reference(section_rows, routes, route_weights, in_gain, gate_up, down, out_gain):
    outputs = []
    closings = []
    for group in range(2):
        layer = moe_layer(section_rows[group], routes[group], route_weights[group], in_gain[group], gate_up[group], down[group])
        residual = layer.astype(jnp.float32)
        closing = (residual * rms_scale(residual)[:, None] * out_gain[group].astype(jnp.float32)[None, :]).astype(jnp.bfloat16)
        outputs.append(layer)
        closings.append(closing)
    layer_out = jnp.stack(outputs, axis=0)
    handed = jnp.stack([closings[1], closings[0]], axis=0)
    return (layer_out, handed)
```

```python
import jax
import jax.numpy as jnp
from jax import lax
from jax.experimental import pallas as pl
from jax.experimental.pallas import tpu as pltpu
from jax.sharding import PartitionSpec as P

MESH = pl.DeviceIdType.MESH
EPS = 1e-06


def looped(count, step, carry=0):
    if count <= 8:
        for at in range(count):
            carry = step(at, carry)
        return carry
    return lax.fori_loop(0, count, step, carry)


def remote(src, dst, send, recv, target):
    return pltpu.make_async_remote_copy(
        src_ref=src,
        dst_ref=dst,
        send_sem=send,
        recv_sem=recv,
        device_id=target,
        device_id_type=MESH,
    )


def kernel(
    share_count,
    x_ref,
    routes_ref,
    rw_ref,
    in_gain_ref,
    out_gain_ref,
    gate_hbm,
    down_hbm,
    lo_ref,
    handed_ref,
    gate_v,
    down_v,
    rows_v,
    lhs_v,
    sq_own,
    sq_far,
    sums_own,
    sums_far,
    hidden_v,
    y_v,
    part_v,
    ret_v,
    gain_own,
    gain_far,
    lo_far,
    tot_own,
    tot_tp,
    tot_far,
    tot_diag,
    gate_sem,
    down_sem,
    rows_send,
    rows_recv,
    ret_send,
    ret_recv,
    sums_send,
    sums_recv,
    small_send,
    small_recv,
):
    n = rows_v.shape[0]
    rows, width = y_v.shape
    near = x_ref.shape[0]
    hidden = down_v.shape[0]
    span = gate_v.shape[1]
    pieces = sums_own.shape[0]
    cut = sums_own.shape[2]
    model = 2 * width
    section = lax.axis_index("section")
    me = lax.axis_index("ep")
    core = lax.axis_index("tp")
    twin = {"tp": 1 - core}
    across = {"section": 1 - section}
    diagonal = {"section": 1 - section, "tp": 1 - core}

    half = pieces // 2

    def columns(at):
        start = (at // 2) * cut + (at % 2) * hidden
        return slice(start, start + cut)

    gate_copies = [
        pltpu.make_async_copy(
            gate_hbm.at[:, columns(at)], gate_v.at[:, columns(at)], gate_sem.at[at]
        )
        for at in range(pieces)
    ]
    down_copies = [
        pltpu.make_async_copy(
            down_hbm.at[at * cut : (at + 1) * cut], down_v.at[at * cut : (at + 1) * cut], down_sem.at[at]
        )
        for at in range(half)
    ]
    for copy in gate_copies + down_copies:
        copy.start()

    barrier = pltpu.get_barrier_semaphore()

    def greet(step, carry):
        pl.semaphore_signal(
            barrier, inc=1, device_id={"ep": (me + 1 + step) % n}, device_id_type=MESH
        )
        return carry

    looped(n - 1, greet)
    for target in (twin, across, diagonal):
        pl.semaphore_signal(barrier, inc=1, device_id=target, device_id_type=MESH)
    gain_own[...] = out_gain_ref[...].astype(jnp.float32)
    rows_v[me] = x_ref[...]
    pl.semaphore_wait(barrier, n + 2)

    def rows_copy(peer):
        return remote(
            x_ref, rows_v.at[me], rows_send.at[peer], rows_recv.at[me], {"ep": peer}
        )

    def rows_arrival(peer):
        return remote(
            x_ref, rows_v.at[peer], rows_send.at[peer], rows_recv.at[peer], {"ep": peer}
        )

    def send_rows(step, carry):
        rows_copy((me + 1 + step) % n).start()
        return carry

    looped(n - 1, send_rows)
    gain_copy = remote(gain_own, gain_far, small_send.at[0], small_recv.at[0], across)
    gain_copy.start()

    def wait_rows(step, carry):
        rows_arrival((me + 1 + step) % n).wait_recv()
        return carry

    looped(n - 1, wait_rows)

    gain = in_gain_ref[...].astype(jnp.float32)
    group = 16 // near

    def build(at, carry):
        block = jnp.concatenate(
            [rows_v[at * group + i].astype(jnp.float32) for i in range(group)], axis=0
        )
        where = pl.ds(at * 16 if isinstance(at, int) else pl.multiple_of(at * 16, 16), 16)
        squares = jnp.sum(block * block, axis=1, keepdims=True)
        sq_own[where, :] = jnp.broadcast_to(squares, (16, 128))
        lhs_v[where, :] = (block * gain).astype(jnp.bfloat16)
        return carry

    looped(n // group, build)
    sq_copy = remote(sq_own, sq_far, small_send.at[1], small_recv.at[1], twin)
    sq_copy.start()

    sums_copies = []
    for at in range(pieces):
        gate_copies[at].wait()
        sums_own[at] = jnp.dot(
            lhs_v[...], gate_v[:, columns(at)], preferred_element_type=jnp.float32
        )
        copy = remote(
            sums_own.at[at], sums_far.at[at], sums_send.at[at], sums_recv.at[at], twin
        )
        copy.start()
        sums_copies.append(copy)

    sq_copy.wait_recv()
    scale = lax.rsqrt((sq_own[:, :1] + sq_far[:, :1]) / model + EPS)
    for at in range(half):
        sums_copies[2 * at].wait_recv()
        sums_copies[2 * at + 1].wait_recv()
        a = (sums_own[2 * at] + sums_far[2 * at]) * scale
        b = (sums_own[2 * at + 1] + sums_far[2 * at + 1]) * scale
        hidden_v[:, at * cut : (at + 1) * cut] = (a / (1.0 + jnp.exp(-a)) * b).astype(
            jnp.bfloat16
        )
    for copy in down_copies:
        copy.wait()

    tile = 512 if width % 512 == 0 else 128
    tiles = width // tile
    bounds = [0, (tiles + 1) // 2 * tile, width]

    def ret_copy(peer, part):
        where = slice(bounds[part], bounds[part + 1])
        return remote(
            part_v.at[peer, :, where],
            ret_v.at[me, :, where],
            ret_send.at[part, peer],
            ret_recv.at[part, me],
            {"ep": peer},
        )

    def ret_arrival(peer, part):
        where = slice(bounds[part], bounds[part + 1])
        return remote(
            part_v.at[peer, :, where],
            ret_v.at[peer, :, where],
            ret_send.at[part, peer],
            ret_recv.at[part, peer],
            {"ep": peer},
        )

    pair = 8 // near
    for part in range(2):
        low, high = bounds[part], bounds[part + 1]
        for start in range(low, high, tile):
            y_v[:, start : start + tile] = jnp.dot(
                hidden_v[...], down_v[:, start : start + tile], preferred_element_type=jnp.float32
            )

        def split(at, carry):
            where = pl.ds(at * 8 if isinstance(at, int) else pl.multiple_of(at * 8, 8), 8)
            block = y_v[where, low:high]
            for i in range(pair):
                part_v[at * pair + i, :, low:high] = block[i * near : (i + 1) * near].astype(
                    jnp.bfloat16
                )
            return carry

        looped(n // pair, split)

        def send_ret(step, carry):
            ret_copy((me + 1 + step) % n, part).start()
            return carry

        looped(n - 1, send_ret)
        ret_v[me, :, low:high] = part_v[me, :, low:high]

    named = routes_ref[...]
    weights = rw_ref[...]
    squares = jnp.zeros((near, 1), jnp.float32)
    for part in range(2):
        low, high = bounds[part], bounds[part + 1]

        def wait_ret(step, carry):
            ret_arrival((me + 1 + step) % n, part).wait_recv()
            return carry

        looped(n - 1, wait_ret)

        def add(at, total):
            weight = jnp.sum(
                jnp.where(named == at // share_count, weights, 0.0), axis=1, keepdims=True
            )
            return total + weight * ret_v[at, :, low:high].astype(jnp.float32)

        mixture = looped(n, add, jnp.zeros((near, high - low), jnp.float32))
        out = (x_ref[:, low:high].astype(jnp.float32) + mixture).astype(jnp.bfloat16)
        lo_ref[:, low:high] = out
        residual = out.astype(jnp.float32)
        squares = squares + jnp.sum(residual * residual, axis=1, keepdims=True)
    tot_own[...] = jnp.broadcast_to(squares, tot_own.shape)
    tail = [
        remote(lo_ref, lo_far, small_send.at[2], small_recv.at[2], across),
        remote(tot_own, tot_far, small_send.at[3], small_recv.at[3], across),
        remote(tot_own, tot_diag, small_send.at[4], small_recv.at[4], diagonal),
    ]
    for copy in tail:
        copy.start()
    gain_copy.wait_recv()
    for copy in tail:
        copy.wait_recv()
    final = lax.rsqrt((tot_far[:, :1] + tot_diag[:, :1]) / model + EPS)
    handed_ref[...] = (lo_far[...].astype(jnp.float32) * final * gain_far[...]).astype(
        jnp.bfloat16
    )

    for copy in [gain_copy, sq_copy] + sums_copies + tail:
        copy.wait_send()

    def drain(step, carry):
        peer = (me + 1 + step) % n
        rows_copy(peer).wait_send()
        for part in range(2):
            ret_copy(peer, part).wait_send()
        return carry

    looped(n - 1, drain)


def body(section_rows, routes, route_weights, in_gain, gate_up, down, out_gain):
    near, width = section_rows.shape[1:]
    hidden = down.shape[2]
    span = gate_up.shape[3]
    n = lax.axis_size("ep")
    share_count = min(16, n // 4)
    rows = n * near
    cut = min(512, hidden)
    pieces = span // cut
    vmem = pl.BlockSpec(memory_space=pltpu.VMEM)
    hbm = pl.BlockSpec(memory_space=pl.ANY)
    f32, bf16 = jnp.float32, jnp.bfloat16
    dma = pltpu.SemaphoreType.DMA
    layer_out, handed = pl.pallas_call(
        lambda *refs: kernel(share_count, *refs),
        out_shape=[jax.ShapeDtypeStruct((near, width), bf16)] * 2,
        in_specs=[vmem] * 5 + [hbm] * 2,
        out_specs=[vmem] * 2,
        scratch_shapes=[
            pltpu.VMEM((width, span), bf16),
            pltpu.VMEM((hidden, width), bf16),
            pltpu.VMEM((n, near, width), bf16),
            pltpu.VMEM((rows, width), bf16),
            pltpu.VMEM((rows, 128), f32),
            pltpu.VMEM((rows, 128), f32),
            pltpu.VMEM((pieces, rows, cut), f32),
            pltpu.VMEM((pieces, rows, cut), f32),
            pltpu.VMEM((rows, hidden), bf16),
            pltpu.VMEM((rows, width), f32),
            pltpu.VMEM((n, near, width), bf16),
            pltpu.VMEM((n, near, width), bf16),
            pltpu.VMEM((1, width), f32),
            pltpu.VMEM((1, width), f32),
            pltpu.VMEM((near, width), bf16),
            pltpu.VMEM((near, 128), f32),
            pltpu.VMEM((near, 128), f32),
            pltpu.VMEM((near, 128), f32),
            pltpu.VMEM((near, 128), f32),
            dma((pieces,)),
            dma((pieces // 2,)),
            dma((n,)),
            dma((n,)),
            dma((2, n)),
            dma((2, n)),
            dma((pieces,)),
            dma((pieces,)),
            dma((5,)),
            dma((5,)),
        ],
        compiler_params=pltpu.CompilerParams(
            collective_id=0, has_side_effects=True, vmem_limit_bytes=56 * 2**20
        ),
        name="routed_layer",
    )(section_rows[0], routes[0], route_weights[0], in_gain, out_gain, gate_up[0, 0], down[0, 0])
    return (layer_out[None], handed[None])


def solution(mesh):
    return jax.shard_map(
        body,
        mesh=mesh,
        in_specs=(
            P("section", "ep", "tp"),
            P("section", "ep", None),
            P("section", "ep", None),
            P("section", "tp"),
            P("section", "ep", "tp", None),
            P("section", "ep", None, "tp"),
            P("section", "tp"),
        ),
        out_specs=(P("section", "ep", "tp"), P("section", "ep", "tp")),
        check_vma=False,
    )
```

```python
import jax
import jax.numpy as jnp
from jax import lax
from jax.experimental import pallas as pl
from jax.experimental.pallas import tpu as pltpu
from jax.sharding import PartitionSpec as P

MESH = pl.DeviceIdType.MESH
EPS = 1e-06


def looped(count, step, carry=0):
    if count <= 8:
        for at in range(count):
            carry = step(at, carry)
        return carry
    return lax.fori_loop(0, count, step, carry)


def remote(src, dst, send, recv, target):
    return pltpu.make_async_remote_copy(
        src_ref=src,
        dst_ref=dst,
        send_sem=send,
        recv_sem=recv,
        device_id=target,
        device_id_type=MESH,
    )


def kernel(
    share_count,
    x_ref,
    routes_ref,
    rw_ref,
    in_gain_ref,
    out_gain_ref,
    gate_hbm,
    down_hbm,
    lo_ref,
    handed_ref,
    gate_v,
    down_v,
    rows_v,
    lhs_v,
    sq_own,
    sq_far,
    sums_own,
    sums_far,
    hidden_v,
    y_v,
    part_v,
    ret_v,
    gain_own,
    gain_far,
    lo_far,
    tot_own,
    weight_v,
    tot_far,
    tot_diag,
    gate_sem,
    down_sem,
    rows_send,
    rows_recv,
    ret_send,
    ret_recv,
    sums_send,
    sums_recv,
    small_send,
    small_recv,
):
    n = rows_v.shape[0]
    rows, width = y_v.shape
    near = x_ref.shape[0]
    hidden = down_v.shape[0]
    span = gate_v.shape[1]
    pieces = sums_own.shape[0]
    cut = sums_own.shape[2]
    model = 2 * width
    section = lax.axis_index("section")
    me = lax.axis_index("ep")
    core = lax.axis_index("tp")
    twin = {"tp": 1 - core}
    across = {"section": 1 - section}
    diagonal = {"section": 1 - section, "tp": 1 - core}

    half = pieces // 2

    def columns(at):
        start = (at // 2) * cut + (at % 2) * hidden
        return slice(start, start + cut)

    gate_copies = [
        pltpu.make_async_copy(
            gate_hbm.at[:, columns(at)], gate_v.at[:, columns(at)], gate_sem.at[at]
        )
        for at in range(pieces)
    ]
    down_copies = [
        pltpu.make_async_copy(
            down_hbm.at[at * cut : (at + 1) * cut], down_v.at[at * cut : (at + 1) * cut], down_sem.at[at]
        )
        for at in range(half)
    ]
    for copy in gate_copies + down_copies:
        copy.start()

    barrier = pltpu.get_barrier_semaphore()

    def greet(step, carry):
        pl.semaphore_signal(
            barrier, inc=1, device_id={"ep": (me + 1 + step) % n}, device_id_type=MESH
        )
        return carry

    looped(n - 1, greet)
    for target in (twin, across, diagonal):
        pl.semaphore_signal(barrier, inc=1, device_id=target, device_id_type=MESH)
    gain_own[...] = out_gain_ref[...].astype(jnp.float32)
    rows_v[me] = x_ref[...]
    named, weights = routes_ref[...], rw_ref[...]
    corner = lax.broadcasted_iota(jnp.int32, (near, near), 0) == lax.broadcasted_iota(
        jnp.int32, (near, near), 1
    )
    for expert in range(weight_v.shape[0]):
        line = jnp.sum(jnp.where(named == expert, weights, 0.0), axis=0, keepdims=True)
        column = jnp.sum(jnp.where(corner, line, 0.0), axis=1, keepdims=True)
        weight_v[expert] = jnp.broadcast_to(column, (near, 128))
    pl.semaphore_wait(barrier, n + 2)

    def rows_copy(peer):
        return remote(
            x_ref, rows_v.at[me], rows_send.at[peer], rows_recv.at[me], {"ep": peer}
        )

    def rows_arrival(peer):
        return remote(
            x_ref, rows_v.at[peer], rows_send.at[peer], rows_recv.at[peer], {"ep": peer}
        )

    def send_rows(step, carry):
        rows_copy((me + 1 + step) % n).start()
        return carry

    looped(n - 1, send_rows)
    gain_copy = remote(gain_own, gain_far, small_send.at[0], small_recv.at[0], across)
    gain_copy.start()

    def wait_rows(step, carry):
        rows_arrival((me + 1 + step) % n).wait_recv()
        return carry

    looped(n - 1, wait_rows)

    gain = in_gain_ref[...].astype(jnp.float32)
    group = 16 // near

    def build(at, carry):
        block = jnp.concatenate(
            [rows_v[at * group + i].astype(jnp.float32) for i in range(group)], axis=0
        )
        where = pl.ds(at * 16 if isinstance(at, int) else pl.multiple_of(at * 16, 16), 16)
        squares = jnp.sum(block * block, axis=1, keepdims=True)
        sq_own[where, :] = jnp.broadcast_to(squares, (16, 128))
        lhs_v[where, :] = (block * gain).astype(jnp.bfloat16)
        return carry

    looped(n // group, build)
    sq_copy = remote(sq_own, sq_far, small_send.at[1], small_recv.at[1], twin)
    sq_copy.start()

    sums_copies = []
    for at in range(pieces):
        gate_copies[at].wait()
        sums_own[at] = jnp.dot(
            lhs_v[...], gate_v[:, columns(at)], preferred_element_type=jnp.float32
        )
        copy = remote(
            sums_own.at[at], sums_far.at[at], sums_send.at[at], sums_recv.at[at], twin
        )
        copy.start()
        sums_copies.append(copy)

    sq_copy.wait_recv()
    scale = lax.rsqrt((sq_own[:, :1] + sq_far[:, :1]) / model + EPS)
    for at in range(half):
        sums_copies[2 * at].wait_recv()
        sums_copies[2 * at + 1].wait_recv()
        a = (sums_own[2 * at] + sums_far[2 * at]) * scale
        b = (sums_own[2 * at + 1] + sums_far[2 * at + 1]) * scale
        hidden_v[:, at * cut : (at + 1) * cut] = (a / (1.0 + jnp.exp(-a)) * b).astype(
            jnp.bfloat16
        )
    for copy in down_copies:
        copy.wait()

    tile = 512 if width % 512 == 0 else 128
    tiles = width // tile
    bounds = [0, (tiles + 1) // 2 * tile, width]

    def ret_copy(peer, part):
        where = slice(bounds[part], bounds[part + 1])
        return remote(
            part_v.at[peer, :, where],
            ret_v.at[me, :, where],
            ret_send.at[part, peer],
            ret_recv.at[part, me],
            {"ep": peer},
        )

    def ret_arrival(peer, part):
        where = slice(bounds[part], bounds[part + 1])
        return remote(
            part_v.at[peer, :, where],
            ret_v.at[peer, :, where],
            ret_send.at[part, peer],
            ret_recv.at[part, peer],
            {"ep": peer},
        )

    pair = 8 // near
    for part in range(2):
        low, high = bounds[part], bounds[part + 1]
        for start in range(low, high, tile):
            y_v[:, start : start + tile] = jnp.dot(
                hidden_v[...], down_v[:, start : start + tile], preferred_element_type=jnp.float32
            )

        def split(at, carry):
            where = pl.ds(at * 8 if isinstance(at, int) else pl.multiple_of(at * 8, 8), 8)
            block = y_v[where, low:high]
            for i in range(pair):
                part_v[at * pair + i, :, low:high] = block[i * near : (i + 1) * near].astype(
                    jnp.bfloat16
                )
            return carry

        looped(n // pair, split)

        def send_ret(step, carry):
            ret_copy((me + 1 + step) % n, part).start()
            return carry

        looped(n - 1, send_ret)
        ret_v[me, :, low:high] = part_v[me, :, low:high]

    squares = jnp.zeros((near, 1), jnp.float32)
    for part in range(2):
        low, high = bounds[part], bounds[part + 1]

        def wait_ret(step, carry):
            ret_arrival((me + 1 + step) % n, part).wait_recv()
            return carry

        looped(n - 1, wait_ret)

        def add(at, total):
            weight = weight_v[at // share_count][:, :1]
            return total + weight * ret_v[at, :, low:high].astype(jnp.float32)

        mixture = looped(n, add, jnp.zeros((near, high - low), jnp.float32))
        out = (x_ref[:, low:high].astype(jnp.float32) + mixture).astype(jnp.bfloat16)
        lo_ref[:, low:high] = out
        residual = out.astype(jnp.float32)
        squares = squares + jnp.sum(residual * residual, axis=1, keepdims=True)
    tot_own[...] = jnp.broadcast_to(squares, tot_own.shape)
    tail = [
        remote(lo_ref, lo_far, small_send.at[2], small_recv.at[2], across),
        remote(tot_own, tot_far, small_send.at[3], small_recv.at[3], across),
        remote(tot_own, tot_diag, small_send.at[4], small_recv.at[4], diagonal),
    ]
    for copy in tail:
        copy.start()
    gain_copy.wait_recv()
    for copy in tail:
        copy.wait_recv()
    final = lax.rsqrt((tot_far[:, :1] + tot_diag[:, :1]) / model + EPS)
    handed_ref[...] = (lo_far[...].astype(jnp.float32) * final * gain_far[...]).astype(
        jnp.bfloat16
    )

    for copy in [gain_copy, sq_copy] + sums_copies + tail:
        copy.wait_send()

    def drain(step, carry):
        peer = (me + 1 + step) % n
        rows_copy(peer).wait_send()
        for part in range(2):
            ret_copy(peer, part).wait_send()
        return carry

    looped(n - 1, drain)


def deliver(lo_ref, handed_ref, lo_out, handed_out, sems):
    copies = [
        pltpu.make_async_copy(lo_ref, lo_out, sems.at[0]),
        pltpu.make_async_copy(handed_ref, handed_out, sems.at[1]),
    ]
    for copy in copies:
        copy.start()
    for copy in copies:
        copy.wait()


def body(section_rows, routes, route_weights, in_gain, gate_up, down, out_gain):
    near, width = section_rows.shape[1:]
    hidden = down.shape[2]
    span = gate_up.shape[3]
    n = lax.axis_size("ep")
    share_count = min(16, n // 4)
    rows = n * near
    cut = min(512, hidden)
    pieces = span // cut
    vmem = pl.BlockSpec(memory_space=pltpu.VMEM)
    hbm = pl.BlockSpec(memory_space=pl.ANY)
    f32, bf16 = jnp.float32, jnp.bfloat16
    dma = pltpu.SemaphoreType.DMA
    layer_out, handed = pl.pallas_call(
        lambda *refs: kernel(share_count, *refs),
        out_shape=[pltpu.VMEM((near, width), bf16)] * 2,
        in_specs=[vmem] * 5 + [hbm] * 2,
        out_specs=[vmem] * 2,
        scratch_shapes=[
            pltpu.VMEM((width, span), bf16),
            pltpu.VMEM((hidden, width), bf16),
            pltpu.VMEM((n, near, width), bf16),
            pltpu.VMEM((rows, width), bf16),
            pltpu.VMEM((rows, 128), f32),
            pltpu.VMEM((rows, 128), f32),
            pltpu.VMEM((pieces, rows, cut), f32),
            pltpu.VMEM((pieces, rows, cut), f32),
            pltpu.VMEM((rows, hidden), bf16),
            pltpu.VMEM((rows, width), f32),
            pltpu.VMEM((n, near, width), bf16),
            pltpu.VMEM((n, near, width), bf16),
            pltpu.VMEM((1, width), f32),
            pltpu.VMEM((1, width), f32),
            pltpu.VMEM((near, width), bf16),
            pltpu.VMEM((near, 128), f32),
            pltpu.VMEM((n // share_count, near, 128), f32),
            pltpu.VMEM((near, 128), f32),
            pltpu.VMEM((near, 128), f32),
            dma((pieces,)),
            dma((pieces // 2,)),
            dma((n,)),
            dma((n,)),
            dma((2, n)),
            dma((2, n)),
            dma((pieces,)),
            dma((pieces,)),
            dma((5,)),
            dma((5,)),
        ],
        compiler_params=pltpu.CompilerParams(
            collective_id=0, has_side_effects=True, vmem_limit_bytes=56 * 2**20
        ),
        name="routed_layer",
    )(section_rows[0], routes[0].T, route_weights[0].T, in_gain, out_gain, gate_up[0, 0], down[0, 0])
    layer_out, handed = pl.pallas_call(
        deliver,
        out_shape=[jax.ShapeDtypeStruct((near, width), bf16)] * 2,
        in_specs=[vmem] * 2,
        out_specs=[hbm] * 2,
        scratch_shapes=[dma((2,))],
        name="deliver",
    )(layer_out, handed)
    return (layer_out[None], handed[None])


def solution(mesh):
    return jax.shard_map(
        body,
        mesh=mesh,
        in_specs=(
            P("section", "ep", "tp"),
            P("section", "ep", None),
            P("section", "ep", None),
            P("section", "tp"),
            P("section", "ep", "tp", None),
            P("section", "ep", None, "tp"),
            P("section", "tp"),
        ),
        out_specs=(P("section", "ep", "tp"), P("section", "ep", "tp")),
        check_vma=False,
    )
```

```python
import jax
import jax.numpy as jnp
from jax import lax
from jax.experimental import pallas as pl
from jax.experimental.pallas import tpu as pltpu
from jax.sharding import PartitionSpec as P

MESH = pl.DeviceIdType.MESH
EPS = 1e-06


def looped(count, step, carry=0):
    if count <= 8:
        for at in range(count):
            carry = step(at, carry)
        return carry
    return lax.fori_loop(0, count, step, carry)


def remote(src, dst, send, recv, target):
    return pltpu.make_async_remote_copy(
        src_ref=src,
        dst_ref=dst,
        send_sem=send,
        recv_sem=recv,
        device_id=target,
        device_id_type=MESH,
    )


def kernel(
    share_count,
    x_hbm,
    routes_hbm,
    rw_hbm,
    in_gain_hbm,
    out_gain_hbm,
    gate_hbm,
    down_hbm,
    lo_ref,
    handed_ref,
    x_ref,
    routes_ref,
    rw_ref,
    in_gain_ref,
    out_gain_ref,
    gate_v,
    down_v,
    rows_v,
    lhs_v,
    sq_own,
    sq_far,
    sums_own,
    sums_far,
    hidden_v,
    y_v,
    own_v,
    part_v,
    half_v,
    sum_v,
    ret_v,
    gain_own,
    gain_far,
    lo_far,
    tot_own,
    weight_v,
    tot_far,
    tot_diag,
    in_sem,
    gate_sem,
    down_sem,
    rows_send,
    rows_recv,
    fwd_send,
    half_send,
    half_recv,
    ret_send,
    ret_recv,
    sums_send,
    sums_recv,
    small_send,
    small_recv,
):
    n = rows_v.shape[0]
    planes = n // 2
    width = y_v.shape[1]
    near = x_ref.shape[0]
    hidden = down_v.shape[0]
    pieces = sums_own.shape[0]
    cut = sums_own.shape[2]
    model = 2 * width
    half = pieces // 2
    section = lax.axis_index("section")
    me = lax.axis_index("ep")
    core = lax.axis_index("tp")
    plane, side = me // 2, me % 2
    buddy = {"ep": me + 1 - 2 * side}
    twin = {"tp": 1 - core}
    across = {"section": 1 - section}
    diagonal = {"section": 1 - section, "tp": 1 - core}

    def others(step, order=None):
        if planes > 8:

            def one(at, carry):
                step((plane + 1 + at) % planes)
                return carry

            lax.fori_loop(0, planes - 1, one, 0)
            return
        for offset in order or range(planes - 1, 0, -1):
            target, bit = plane, 1
            while bit < planes:
                if offset & bit:
                    target = target + bit * (1 - 2 * ((plane // bit) % 2))
                bit *= 2
            step(target)

    x_copy = pltpu.make_async_copy(x_hbm, x_ref, in_sem.at[0])
    in_copies = [
        pltpu.make_async_copy(routes_hbm, routes_ref, in_sem.at[1]),
        pltpu.make_async_copy(rw_hbm, rw_ref, in_sem.at[2]),
        pltpu.make_async_copy(in_gain_hbm, in_gain_ref, in_sem.at[3]),
        pltpu.make_async_copy(out_gain_hbm, out_gain_ref, in_sem.at[4]),
    ]
    x_copy.start()
    for copy in in_copies:
        copy.start()

    barrier = pltpu.get_barrier_semaphore()

    def greet(target):
        pl.semaphore_signal(barrier, inc=1, device_id=target, device_id_type=MESH)

    others(lambda to: greet({"ep": to * 2 + side}))
    for target in (buddy, twin, across, diagonal):
        greet(target)

    def columns(at):
        start = (at // 2) * cut + (at % 2) * hidden
        return slice(start, start + cut)

    gate_copies = [
        pltpu.make_async_copy(
            gate_hbm.at[:, columns(at)], gate_v.at[:, columns(at)], gate_sem.at[at]
        )
        for at in range(pieces)
    ]
    down_copies = [
        pltpu.make_async_copy(
            down_hbm.at[at * cut : (at + 1) * cut], down_v.at[at * cut : (at + 1) * cut], down_sem.at[at]
        )
        for at in range(half)
    ]
    for copy in gate_copies + down_copies:
        copy.start()
    x_copy.wait()
    pl.semaphore_wait(barrier, planes + 3)

    def rows_copy(to):
        return remote(
            x_ref, rows_v.at[me], rows_send.at[to], rows_recv.at[me], {"ep": to * 2 + side}
        )

    def rows_arrival(of, side_of):
        slot = of * 2 + side_of
        return remote(x_ref, rows_v.at[slot], rows_send.at[of], rows_recv.at[slot], buddy)

    def forward(of):
        slot = of * 2 + side
        return remote(
            rows_v.at[slot], rows_v.at[slot], fwd_send.at[of], rows_recv.at[slot], buddy
        )

    own_copy = remote(x_ref, rows_v.at[me], fwd_send.at[plane], rows_recv.at[me], buddy)
    others(lambda to: rows_copy(to).start())
    own_copy.start()
    rows_v[me] = x_ref[...]
    for copy in in_copies:
        copy.wait()
    gain_own[...] = out_gain_ref[...].astype(jnp.float32)
    gain_copy = remote(gain_own, gain_far, small_send.at[0], small_recv.at[0], across)
    gain_copy.start()

    def pass_on(of):
        rows_arrival(of, side).wait_recv()
        forward(of).start()

    early = [3, 1, 2] if planes == 4 else None
    others(pass_on, early)

    named, weights = routes_ref[...], rw_ref[...]
    corner = lax.broadcasted_iota(jnp.int32, (near, near), 0) == lax.broadcasted_iota(
        jnp.int32, (near, near), 1
    )
    for expert in range(weight_v.shape[0]):
        line = jnp.sum(jnp.where(named == expert, weights, 0.0), axis=0, keepdims=True)
        column = jnp.sum(jnp.where(corner, line, 0.0), axis=1, keepdims=True)
        weight_v[expert] = jnp.broadcast_to(column, (near, 128))

    rows_arrival(plane, 1 - side).wait_recv()
    others(lambda of: rows_arrival(of, 1 - side).wait_recv(), early)

    gain = in_gain_ref[...].astype(jnp.float32)
    group = 16 // near

    def build(at, carry):
        block = jnp.concatenate(
            [rows_v[at * group + i].astype(jnp.float32) for i in range(group)], axis=0
        )
        where = pl.ds(at * 16 if isinstance(at, int) else pl.multiple_of(at * 16, 16), 16)
        squares = jnp.sum(block * block, axis=1, keepdims=True)
        sq_own[where, :] = jnp.broadcast_to(squares, (16, 128))
        lhs_v[where, :] = (block * gain).astype(jnp.bfloat16)
        return carry

    looped(n // group, build)
    sq_copy = remote(sq_own, sq_far, small_send.at[1], small_recv.at[1], twin)
    sq_copy.start()

    sums_copies = []
    for at in range(pieces):
        gate_copies[at].wait()
        sums_own[at] = jnp.dot(
            lhs_v[...], gate_v[:, columns(at)], preferred_element_type=jnp.float32
        )
        copy = remote(
            sums_own.at[at], sums_far.at[at], sums_send.at[at], sums_recv.at[at], twin
        )
        copy.start()
        sums_copies.append(copy)

    sq_copy.wait_recv()
    scale = lax.rsqrt((sq_own[:, :1] + sq_far[:, :1]) / model + EPS)
    for at in range(half):
        sums_copies[2 * at].wait_recv()
        sums_copies[2 * at + 1].wait_recv()
        a = (sums_own[2 * at] + sums_far[2 * at]) * scale
        b = (sums_own[2 * at + 1] + sums_far[2 * at + 1]) * scale
        hidden_v[:, at * cut : (at + 1) * cut] = (a / (1.0 + jnp.exp(-a)) * b).astype(
            jnp.bfloat16
        )
    for copy in down_copies:
        copy.wait()

    tile = 512 if width % 512 == 0 else 128
    tiles = width // tile
    bounds = [0, (tiles + 1) // 2 * tile, width]

    def half_copy(to, part):
        where = slice(bounds[part], bounds[part + 1])
        return remote(
            part_v.at[to, :, where],
            half_v.at[to, :, where],
            half_send.at[part, to],
            half_recv.at[part, to],
            buddy,
        )

    def ret_copy(to, part):
        where = slice(bounds[part], bounds[part + 1])
        return remote(
            sum_v.at[to, :, where],
            ret_v.at[plane, :, where],
            ret_send.at[part, to],
            ret_recv.at[part, plane],
            {"ep": to * 2 + side},
        )

    def ret_arrival(of, part):
        where = slice(bounds[part], bounds[part + 1])
        return remote(
            sum_v.at[of, :, where],
            ret_v.at[of, :, where],
            ret_send.at[part, of],
            ret_recv.at[part, of],
            {"ep": of * 2 + side},
        )

    for part in range(2):
        low, high = bounds[part], bounds[part + 1]
        for start in range(low, high, tile):
            y_v[:, start : start + tile] = jnp.dot(
                hidden_v[...], down_v[:, start : start + tile], preferred_element_type=jnp.float32
            )

        def split(at, carry):
            first = at * 2 * near
            where = pl.ds(
                first if isinstance(at, int) else pl.multiple_of(first, 2 * near), 2 * near
            )
            block = y_v[where, low:high]
            even, odd = block[:near], block[near:]
            own_v[at, :, low:high] = jnp.where(side == 0, even, odd)
            part_v[at, :, low:high] = jnp.where(side == 0, odd, even).astype(jnp.bfloat16)
            return carry

        looped(planes, split)
        others(lambda to: half_copy(to, part).start())
        half_copy(plane, part).start()

    for part in range(2):
        low, high = bounds[part], bounds[part + 1]

        def joined(to):
            half_copy(to, part).wait_recv()
            return (own_v[to, :, low:high] + half_v[to, :, low:high].astype(jnp.float32)).astype(
                jnp.bfloat16
            )

        def send_sum(to):
            sum_v[to, :, low:high] = joined(to)
            ret_copy(to, part).start()

        others(send_sum)
        ret_v[plane, :, low:high] = joined(plane)

    squares = jnp.zeros((near, 1), jnp.float32)
    for part in range(2):
        low, high = bounds[part], bounds[part + 1]
        others(lambda of: ret_arrival(of, part).wait_recv(), early)

        def add(at, total):
            weight = weight_v[at // (share_count // 2)][:, :1]
            return total + weight * ret_v[at, :, low:high].astype(jnp.float32)

        mixture = looped(planes, add, jnp.zeros((near, high - low), jnp.float32))
        out = (x_ref[:, low:high].astype(jnp.float32) + mixture).astype(jnp.bfloat16)
        lo_ref[:, low:high] = out
        residual = out.astype(jnp.float32)
        squares = squares + jnp.sum(residual * residual, axis=1, keepdims=True)
    tot_own[...] = jnp.broadcast_to(squares, tot_own.shape)
    tail = [
        remote(lo_ref, lo_far, small_send.at[2], small_recv.at[2], across),
        remote(tot_own, tot_far, small_send.at[3], small_recv.at[3], across),
        remote(tot_own, tot_diag, small_send.at[4], small_recv.at[4], diagonal),
    ]
    for copy in tail:
        copy.start()
    gain_copy.wait_recv()
    for copy in tail:
        copy.wait_recv()
    final = lax.rsqrt((tot_far[:, :1] + tot_diag[:, :1]) / model + EPS)
    handed_ref[...] = (lo_far[...].astype(jnp.float32) * final * gain_far[...]).astype(
        jnp.bfloat16
    )

    for copy in [gain_copy, sq_copy, own_copy] + sums_copies + tail:
        copy.wait_send()

    def drain(to):
        rows_copy(to).wait_send()
        forward(to).wait_send()
        for part in range(2):
            half_copy(to, part).wait_send()
            ret_copy(to, part).wait_send()

    others(drain)
    for part in range(2):
        half_copy(plane, part).wait_send()


def deliver(lo_ref, handed_ref, lo_out, handed_out, sems):
    copies = [
        pltpu.make_async_copy(lo_ref, lo_out, sems.at[0]),
        pltpu.make_async_copy(handed_ref, handed_out, sems.at[1]),
    ]
    for copy in copies:
        copy.start()
    for copy in copies:
        copy.wait()


def body(section_rows, routes, route_weights, in_gain, gate_up, down, out_gain):
    near, width = section_rows.shape[1:]
    hidden = down.shape[2]
    topk = routes.shape[2]
    span = gate_up.shape[3]
    n = lax.axis_size("ep")
    share_count = min(16, n // 4)
    rows = n * near
    cut = min(512, hidden)
    pieces = span // cut
    vmem = pl.BlockSpec(memory_space=pltpu.VMEM)
    hbm = pl.BlockSpec(memory_space=pl.ANY)
    f32, bf16 = jnp.float32, jnp.bfloat16
    dma = pltpu.SemaphoreType.DMA
    layer_out, handed = pl.pallas_call(
        lambda *refs: kernel(share_count, *refs),
        out_shape=[pltpu.VMEM((near, width), bf16)] * 2,
        in_specs=[hbm] * 7,
        out_specs=[vmem] * 2,
        scratch_shapes=[
            pltpu.VMEM((near, width), bf16),
            pltpu.VMEM((topk, near), jnp.int32),
            pltpu.VMEM((topk, near), f32),
            pltpu.VMEM((1, width), bf16),
            pltpu.VMEM((1, width), bf16),
            pltpu.VMEM((width, span), bf16),
            pltpu.VMEM((hidden, width), bf16),
            pltpu.VMEM((n, near, width), bf16),
            pltpu.VMEM((rows, width), bf16),
            pltpu.VMEM((rows, 128), f32),
            pltpu.VMEM((rows, 128), f32),
            pltpu.VMEM((pieces, rows, cut), f32),
            pltpu.VMEM((pieces, rows, cut), f32),
            pltpu.VMEM((rows, hidden), bf16),
            pltpu.VMEM((rows, width), f32),
            pltpu.VMEM((n // 2, near, width), f32),
            pltpu.VMEM((n // 2, near, width), bf16),
            pltpu.VMEM((n // 2, near, width), bf16),
            pltpu.VMEM((n // 2, near, width), bf16),
            pltpu.VMEM((n // 2, near, width), bf16),
            pltpu.VMEM((1, width), f32),
            pltpu.VMEM((1, width), f32),
            pltpu.VMEM((near, width), bf16),
            pltpu.VMEM((near, 128), f32),
            pltpu.VMEM((n // share_count, near, 128), f32),
            pltpu.VMEM((near, 128), f32),
            pltpu.VMEM((near, 128), f32),
            dma((5,)),
            dma((pieces,)),
            dma((pieces // 2,)),
            dma((n // 2,)),
            dma((n,)),
            dma((n // 2,)),
            dma((2, n // 2)),
            dma((2, n // 2)),
            dma((2, n // 2)),
            dma((2, n // 2)),
            dma((pieces,)),
            dma((pieces,)),
            dma((5,)),
            dma((5,)),
        ],
        compiler_params=pltpu.CompilerParams(
            collective_id=0, has_side_effects=True, vmem_limit_bytes=60 * 2**20
        ),
        name="routed_layer",
    )(section_rows[0], routes[0].T, route_weights[0].T, in_gain, out_gain, gate_up[0, 0], down[0, 0])
    layer_out, handed = pl.pallas_call(
        deliver,
        out_shape=[jax.ShapeDtypeStruct((near, width), bf16)] * 2,
        in_specs=[vmem] * 2,
        out_specs=[hbm] * 2,
        scratch_shapes=[dma((2,))],
        compiler_params=pltpu.CompilerParams(vmem_limit_bytes=2 * 2**20),
        name="deliver",
    )(layer_out, handed)
    return (layer_out[None], handed[None])


def solution(mesh):
    return jax.shard_map(
        body,
        mesh=mesh,
        in_specs=(
            P("section", "ep", "tp"),
            P("section", "ep", None),
            P("section", "ep", None),
            P("section", "tp"),
            P("section", "ep", "tp", None),
            P("section", "ep", None, "tp"),
            P("section", "tp"),
        ),
        out_specs=(P("section", "ep", "tp"), P("section", "ep", "tp")),
        check_vma=False,
    )
```

```python
import jax
import jax.numpy as jnp
from jax import lax
from jax.experimental import pallas as pl
from jax.experimental.pallas import tpu as pltpu
from jax.sharding import PartitionSpec as P

MESH = pl.DeviceIdType.MESH
EPS = 1e-06


def looped(count, step, carry=0):
    if count <= 8:
        for at in range(count):
            carry = step(at, carry)
        return carry
    return lax.fori_loop(0, count, step, carry)


def remote(src, dst, send, recv, target):
    return pltpu.make_async_remote_copy(
        src_ref=src,
        dst_ref=dst,
        send_sem=send,
        recv_sem=recv,
        device_id=target,
        device_id_type=MESH,
    )


def kernel(
    share_count,
    x_hbm,
    routes_hbm,
    rw_hbm,
    in_gain_hbm,
    out_gain_hbm,
    gate_hbm,
    down_hbm,
    lo_ref,
    handed_ref,
    x_ref,
    routes_ref,
    rw_ref,
    in_gain_ref,
    out_gain_ref,
    gate_v,
    down_v,
    rows_v,
    lhs_v,
    sq_own,
    sq_far,
    sums_own,
    sums_far,
    hidden_v,
    y_v,
    own_v,
    part_v,
    half_v,
    sum_v,
    ret_v,
    gain_own,
    gain_far,
    lo_far,
    tot_own,
    weight_v,
    tot_far,
    tot_diag,
    in_sem,
    gate_sem,
    down_sem,
    rows_send,
    rows_recv,
    fwd_send,
    half_send,
    half_recv,
    ret_send,
    ret_recv,
    sums_send,
    sums_recv,
    small_send,
    small_recv,
    lo_send,
    lo_recv,
):
    n = rows_v.shape[0]
    planes = n // 2
    width = y_v.shape[1]
    near = x_ref.shape[0]
    hidden = down_v.shape[0]
    pieces = sums_own.shape[0]
    cut = sums_own.shape[2]
    model = 2 * width
    half = pieces // 2
    section = lax.axis_index("section")
    me = lax.axis_index("ep")
    core = lax.axis_index("tp")
    plane, side = me // 2, me % 2
    buddy = {"ep": me + 1 - 2 * side}
    twin = {"tp": 1 - core}
    across = {"section": 1 - section}
    diagonal = {"section": 1 - section, "tp": 1 - core}

    def others(step, order=None):
        if planes > 8:

            def one(at, carry):
                step((plane + 1 + at) % planes)
                return carry

            lax.fori_loop(0, planes - 1, one, 0)
            return
        for offset in order or range(planes - 1, 0, -1):
            target, bit = plane, 1
            while bit < planes:
                if offset & bit:
                    target = target + bit * (1 - 2 * ((plane // bit) % 2))
                bit *= 2
            step(target)

    x_copy = pltpu.make_async_copy(x_hbm, x_ref, in_sem.at[0])
    in_copies = [
        pltpu.make_async_copy(routes_hbm, routes_ref, in_sem.at[1]),
        pltpu.make_async_copy(rw_hbm, rw_ref, in_sem.at[2]),
        pltpu.make_async_copy(in_gain_hbm, in_gain_ref, in_sem.at[3]),
        pltpu.make_async_copy(out_gain_hbm, out_gain_ref, in_sem.at[4]),
    ]
    x_copy.start()
    for copy in in_copies:
        copy.start()

    barrier = pltpu.get_barrier_semaphore()

    def greet(target):
        pl.semaphore_signal(barrier, inc=1, device_id=target, device_id_type=MESH)

    others(lambda to: greet({"ep": to * 2 + side}))
    for target in (buddy, twin, across, diagonal):
        greet(target)

    def columns(at):
        start = (at // 2) * cut + (at % 2) * hidden
        return slice(start, start + cut)

    gate_copies = [
        pltpu.make_async_copy(
            gate_hbm.at[:, columns(at)], gate_v.at[:, columns(at)], gate_sem.at[at]
        )
        for at in range(pieces)
    ]
    down_copies = [
        pltpu.make_async_copy(
            down_hbm.at[at * cut : (at + 1) * cut], down_v.at[at * cut : (at + 1) * cut], down_sem.at[at]
        )
        for at in range(half)
    ]
    for copy in gate_copies + down_copies:
        copy.start()
    x_copy.wait()
    pl.semaphore_wait(barrier, planes + 3)

    def rows_copy(to):
        return remote(
            x_ref, rows_v.at[me], rows_send.at[to], rows_recv.at[me], {"ep": to * 2 + side}
        )

    def rows_arrival(of, side_of):
        slot = of * 2 + side_of
        return remote(x_ref, rows_v.at[slot], rows_send.at[of], rows_recv.at[slot], buddy)

    def forward(of):
        slot = of * 2 + side
        return remote(
            rows_v.at[slot], rows_v.at[slot], fwd_send.at[of], rows_recv.at[slot], buddy
        )

    own_copy = remote(x_ref, rows_v.at[me], fwd_send.at[plane], rows_recv.at[me], buddy)
    others(lambda to: rows_copy(to).start())
    own_copy.start()
    rows_v[me] = x_ref[...]
    for copy in in_copies:
        copy.wait()
    gain_own[...] = out_gain_ref[...].astype(jnp.float32)
    gain_copy = remote(gain_own, gain_far, small_send.at[0], small_recv.at[0], across)
    gain_copy.start()

    def pass_on(of):
        rows_arrival(of, side).wait_recv()
        forward(of).start()

    early = [3, 1, 2] if planes == 4 else None
    others(pass_on, early)

    named, weights = routes_ref[...], rw_ref[...]
    corner = lax.broadcasted_iota(jnp.int32, (near, near), 0) == lax.broadcasted_iota(
        jnp.int32, (near, near), 1
    )
    for expert in range(weight_v.shape[0]):
        line = jnp.sum(jnp.where(named == expert, weights, 0.0), axis=0, keepdims=True)
        column = jnp.sum(jnp.where(corner, line, 0.0), axis=1, keepdims=True)
        weight_v[expert] = jnp.broadcast_to(column, (near, 128))

    gain = in_gain_ref[...].astype(jnp.float32)
    group = 16 // near

    def build(at, carry=0):
        block = jnp.concatenate(
            [rows_v[at * group + i].astype(jnp.float32) for i in range(group)], axis=0
        )
        where = pl.ds(at * 16 if isinstance(at, int) else pl.multiple_of(at * 16, 16), 16)
        squares = jnp.sum(block * block, axis=1, keepdims=True)
        sq_own[where, :] = jnp.broadcast_to(squares, (16, 128))
        lhs_v[where, :] = (block * gain).astype(jnp.bfloat16)
        return carry

    def wait_far(of):
        rows_arrival(of, 1 - side).wait_recv()

    wait_far(plane)
    if n // group == 2 and planes == 4:
        others(wait_far, [1])
        build(plane // 2)
        others(wait_far, [3, 2])
        build(1 - plane // 2)
    else:
        others(wait_far)
        looped(n // group, build)
    sq_copy = remote(sq_own, sq_far, small_send.at[1], small_recv.at[1], twin)
    sq_copy.start()

    sums_copies = []
    for at in range(pieces):
        gate_copies[at].wait()
        sums_own[at] = jnp.dot(
            lhs_v[...], gate_v[:, columns(at)], preferred_element_type=jnp.float32
        )
        copy = remote(
            sums_own.at[at], sums_far.at[at], sums_send.at[at], sums_recv.at[at], twin
        )
        copy.start()
        sums_copies.append(copy)

    tile = 512 if width % 512 == 0 else 128
    third = max(1, width // tile * 3 // 7) * tile
    bounds = [0, third, 2 * third, width]
    parts = len(bounds) - 1

    def down_step(at, start):
        term = jnp.dot(
            hidden_v[:, at * cut : (at + 1) * cut],
            down_v[at * cut : (at + 1) * cut, start : start + tile],
            preferred_element_type=jnp.float32,
        )
        where = slice(start, start + tile)
        y_v[:, where] = term if at == 0 else y_v[:, where] + term

    sq_copy.wait_recv()
    scale = lax.rsqrt((sq_own[:, :1] + sq_far[:, :1]) / model + EPS)
    for at in range(half):
        sums_copies[2 * at].wait_recv()
        sums_copies[2 * at + 1].wait_recv()
        a = (sums_own[2 * at] + sums_far[2 * at]) * scale
        b = (sums_own[2 * at + 1] + sums_far[2 * at + 1]) * scale
        hidden_v[:, at * cut : (at + 1) * cut] = (a / (1.0 + jnp.exp(-a)) * b).astype(
            jnp.bfloat16
        )
        down_copies[at].wait()
        if at < half - 1:
            for start in range(0, width, tile):
                down_step(at, start)

    def half_copy(to, part):
        where = slice(bounds[part], bounds[part + 1])
        return remote(
            part_v.at[to, :, where],
            half_v.at[to, :, where],
            half_send.at[part, to],
            half_recv.at[part, to],
            buddy,
        )

    def ret_copy(to, part):
        where = slice(bounds[part], bounds[part + 1])
        return remote(
            sum_v.at[to, :, where],
            ret_v.at[plane, :, where],
            ret_send.at[part, to],
            ret_recv.at[part, plane],
            {"ep": to * 2 + side},
        )

    def ret_arrival(of, part):
        where = slice(bounds[part], bounds[part + 1])
        return remote(
            sum_v.at[of, :, where],
            ret_v.at[of, :, where],
            ret_send.at[part, of],
            ret_recv.at[part, of],
            {"ep": of * 2 + side},
        )

    def produce(part):
        low, high = bounds[part], bounds[part + 1]
        for start in range(low, high, tile):
            down_step(half - 1, start)

        def split(at, carry):
            first = at * 2 * near
            where = pl.ds(
                first if isinstance(at, int) else pl.multiple_of(first, 2 * near), 2 * near
            )
            block = y_v[where, low:high]
            even, odd = block[:near], block[near:]
            own_v[at, :, low:high] = jnp.where(side == 0, even, odd)
            part_v[at, :, low:high] = jnp.where(side == 0, odd, even).astype(jnp.bfloat16)
            return carry

        looped(planes, split)
        others(lambda to: half_copy(to, part).start())
        half_copy(plane, part).start()

    def combine(part):
        low, high = bounds[part], bounds[part + 1]

        def joined(to):
            half_copy(to, part).wait_recv()
            return (own_v[to, :, low:high] + half_v[to, :, low:high].astype(jnp.float32)).astype(
                jnp.bfloat16
            )

        def send_sum(to):
            sum_v[to, :, low:high] = joined(to)
            ret_copy(to, part).start()

        others(send_sum)
        ret_v[plane, :, low:high] = joined(plane)

    for part in range(parts):
        produce(part)
        if part > 0:
            combine(part - 1)
    combine(parts - 1)

    def lo_copy(part):
        where = slice(bounds[part], bounds[part + 1])
        return remote(
            lo_ref.at[:, where], lo_far.at[:, where], lo_send.at[part], lo_recv.at[part], across
        )

    squares = jnp.zeros((near, 1), jnp.float32)
    for part in range(parts):
        low, high = bounds[part], bounds[part + 1]
        others(lambda of: ret_arrival(of, part).wait_recv(), early)

        def add(at, total):
            weight = weight_v[at // (share_count // 2)][:, :1]
            return total + weight * ret_v[at, :, low:high].astype(jnp.float32)

        mixture = looped(planes, add, jnp.zeros((near, high - low), jnp.float32))
        out = (x_ref[:, low:high].astype(jnp.float32) + mixture).astype(jnp.bfloat16)
        lo_ref[:, low:high] = out
        lo_copy(part).start()
        residual = out.astype(jnp.float32)
        squares = squares + jnp.sum(residual * residual, axis=1, keepdims=True)
    tot_own[...] = jnp.broadcast_to(squares, tot_own.shape)
    tail = [
        remote(tot_own, tot_far, small_send.at[2], small_recv.at[2], across),
        remote(tot_own, tot_diag, small_send.at[3], small_recv.at[3], diagonal),
    ]
    for copy in tail:
        copy.start()
    gain_copy.wait_recv()
    for copy in tail:
        copy.wait_recv()
    for part in range(parts):
        lo_copy(part).wait_recv()
    final = lax.rsqrt((tot_far[:, :1] + tot_diag[:, :1]) / model + EPS)
    handed_ref[...] = (lo_far[...].astype(jnp.float32) * final * gain_far[...]).astype(
        jnp.bfloat16
    )

    for copy in [gain_copy, sq_copy, own_copy] + sums_copies + tail:
        copy.wait_send()

    def drain(to):
        rows_copy(to).wait_send()
        forward(to).wait_send()
        for part in range(parts):
            half_copy(to, part).wait_send()
            ret_copy(to, part).wait_send()

    others(drain)
    for part in range(parts):
        half_copy(plane, part).wait_send()
        lo_copy(part).wait_send()


def deliver(lo_ref, handed_ref, lo_out, handed_out, sems):
    copies = [
        pltpu.make_async_copy(lo_ref, lo_out, sems.at[0]),
        pltpu.make_async_copy(handed_ref, handed_out, sems.at[1]),
    ]
    for copy in copies:
        copy.start()
    for copy in copies:
        copy.wait()


def body(section_rows, routes, route_weights, in_gain, gate_up, down, out_gain):
    near, width = section_rows.shape[1:]
    hidden = down.shape[2]
    topk = routes.shape[2]
    span = gate_up.shape[3]
    n = lax.axis_size("ep")
    share_count = min(16, n // 4)
    rows = n * near
    cut = min(512, hidden)
    pieces = span // cut
    vmem = pl.BlockSpec(memory_space=pltpu.VMEM)
    hbm = pl.BlockSpec(memory_space=pl.ANY)
    f32, bf16 = jnp.float32, jnp.bfloat16
    dma = pltpu.SemaphoreType.DMA
    layer_out, handed = pl.pallas_call(
        lambda *refs: kernel(share_count, *refs),
        out_shape=[pltpu.VMEM((near, width), bf16)] * 2,
        in_specs=[hbm] * 7,
        out_specs=[vmem] * 2,
        scratch_shapes=[
            pltpu.VMEM((near, width), bf16),
            pltpu.VMEM((topk, near), jnp.int32),
            pltpu.VMEM((topk, near), f32),
            pltpu.VMEM((1, width), bf16),
            pltpu.VMEM((1, width), bf16),
            pltpu.VMEM((width, span), bf16),
            pltpu.VMEM((hidden, width), bf16),
            pltpu.VMEM((n, near, width), bf16),
            pltpu.VMEM((rows, width), bf16),
            pltpu.VMEM((rows, 128), f32),
            pltpu.VMEM((rows, 128), f32),
            pltpu.VMEM((pieces, rows, cut), f32),
            pltpu.VMEM((pieces, rows, cut), f32),
            pltpu.VMEM((rows, hidden), bf16),
            pltpu.VMEM((rows, width), f32),
            pltpu.VMEM((n // 2, near, width), f32),
            pltpu.VMEM((n // 2, near, width), bf16),
            pltpu.VMEM((n // 2, near, width), bf16),
            pltpu.VMEM((n // 2, near, width), bf16),
            pltpu.VMEM((n // 2, near, width), bf16),
            pltpu.VMEM((1, width), f32),
            pltpu.VMEM((1, width), f32),
            pltpu.VMEM((near, width), bf16),
            pltpu.VMEM((near, 128), f32),
            pltpu.VMEM((n // share_count, near, 128), f32),
            pltpu.VMEM((near, 128), f32),
            pltpu.VMEM((near, 128), f32),
            dma((5,)),
            dma((pieces,)),
            dma((pieces // 2,)),
            dma((n // 2,)),
            dma((n,)),
            dma((n // 2,)),
            dma((3, n // 2)),
            dma((3, n // 2)),
            dma((3, n // 2)),
            dma((3, n // 2)),
            dma((pieces,)),
            dma((pieces,)),
            dma((4,)),
            dma((4,)),
            dma((3,)),
            dma((3,)),
        ],
        compiler_params=pltpu.CompilerParams(
            collective_id=0, has_side_effects=True, vmem_limit_bytes=60 * 2**20
        ),
        name="routed_layer",
    )(section_rows[0], routes[0].T, route_weights[0].T, in_gain, out_gain, gate_up[0, 0], down[0, 0])
    layer_out, handed = pl.pallas_call(
        deliver,
        out_shape=[jax.ShapeDtypeStruct((near, width), bf16)] * 2,
        in_specs=[vmem] * 2,
        out_specs=[hbm] * 2,
        scratch_shapes=[dma((2,))],
        compiler_params=pltpu.CompilerParams(vmem_limit_bytes=2 * 2**20),
        name="deliver",
    )(layer_out, handed)
    return (layer_out[None], handed[None])


def solution(mesh):
    return jax.shard_map(
        body,
        mesh=mesh,
        in_specs=(
            P("section", "ep", "tp"),
            P("section", "ep", None),
            P("section", "ep", None),
            P("section", "tp"),
            P("section", "ep", "tp", None),
            P("section", "ep", None, "tp"),
            P("section", "tp"),
        ),
        out_specs=(P("section", "ep", "tp"), P("section", "ep", "tp")),
        check_vma=False,
    )
```

```python
import jax
import jax.numpy as jnp
from jax import lax
from jax.experimental import pallas as pl
from jax.experimental.pallas import tpu as pltpu
from jax.sharding import PartitionSpec as P

MESH = pl.DeviceIdType.MESH
EPS = 1e-06


def looped(count, step, carry=0):
    if count <= 8:
        for at in range(count):
            carry = step(at, carry)
        return carry
    return lax.fori_loop(0, count, step, carry)


def remote(src, dst, send, recv, target):
    return pltpu.make_async_remote_copy(
        src_ref=src,
        dst_ref=dst,
        send_sem=send,
        recv_sem=recv,
        device_id=target,
        device_id_type=MESH,
    )


def kernel(
    share_count,
    x_hbm,
    routes_hbm,
    rw_hbm,
    in_gain_hbm,
    out_gain_hbm,
    gate_hbm,
    down_hbm,
    lo_ref,
    handed_ref,
    x_ref,
    routes_ref,
    rw_ref,
    in_gain_ref,
    out_gain_ref,
    gate_v,
    down_v,
    rows_v,
    lhs_v,
    sums_own,
    sums_far,
    hidden_v,
    y_v,
    own_v,
    part_v,
    half_v,
    sum_v,
    ret_v,
    gain_own,
    gain_far,
    lo_far,
    tot_own,
    weight_v,
    tot_far,
    tot_diag,
    in_sem,
    gate_sem,
    down_sem,
    rows_send,
    rows_recv,
    fwd_send,
    half_send,
    half_recv,
    ret_send,
    ret_recv,
    sums_send,
    sums_recv,
    small_send,
    small_recv,
):
    n = rows_v.shape[0]
    planes = n // 2
    width = y_v.shape[1]
    near = x_ref.shape[0]
    hidden = down_v.shape[0]
    pieces = 2 * sums_own.shape[0]
    cut = hidden // sums_own.shape[0]
    model = 2 * width
    half = pieces // 2
    section = lax.axis_index("section")
    me = lax.axis_index("ep")
    core = lax.axis_index("tp")
    plane, side = me // 2, me % 2
    buddy = {"ep": me + 1 - 2 * side}
    twin = {"tp": 1 - core}
    across = {"section": 1 - section}
    diagonal = {"section": 1 - section, "tp": 1 - core}

    def others(step, order=None):
        if planes > 8:

            def one(at, carry):
                step((plane + 1 + at) % planes)
                return carry

            lax.fori_loop(0, planes - 1, one, 0)
            return
        for offset in order or range(planes - 1, 0, -1):
            target, bit = plane, 1
            while bit < planes:
                if offset & bit:
                    target = target + bit * (1 - 2 * ((plane // bit) % 2))
                bit *= 2
            step(target)

    x_copy = pltpu.make_async_copy(x_hbm, x_ref, in_sem.at[0])
    in_copies = [
        pltpu.make_async_copy(routes_hbm, routes_ref, in_sem.at[1]),
        pltpu.make_async_copy(rw_hbm, rw_ref, in_sem.at[2]),
        pltpu.make_async_copy(in_gain_hbm, in_gain_ref, in_sem.at[3]),
        pltpu.make_async_copy(out_gain_hbm, out_gain_ref, in_sem.at[4]),
    ]
    x_copy.start()
    for copy in in_copies:
        copy.start()

    barrier = pltpu.get_barrier_semaphore()

    def greet(target):
        pl.semaphore_signal(barrier, inc=1, device_id=target, device_id_type=MESH)

    others(lambda to: greet({"ep": to * 2 + side}))
    for target in (buddy, twin, across, diagonal):
        greet(target)

    def columns(at):
        start = (at // 2) * cut + (at % 2) * hidden
        return slice(start, start + cut)

    gate_copies = [
        pltpu.make_async_copy(
            gate_hbm.at[:, columns(at)], gate_v.at[:, columns(at)], gate_sem.at[at]
        )
        for at in range(pieces)
    ]
    down_copies = [
        pltpu.make_async_copy(
            down_hbm.at[at * cut : (at + 1) * cut], down_v.at[at * cut : (at + 1) * cut], down_sem.at[at]
        )
        for at in range(half)
    ]
    for copy in gate_copies + down_copies:
        copy.start()
    x_copy.wait()
    pl.semaphore_wait(barrier, planes + 3)

    def rows_copy(to):
        return remote(
            x_ref, rows_v.at[me], rows_send.at[to], rows_recv.at[me], {"ep": to * 2 + side}
        )

    def rows_arrival(of, side_of):
        slot = of * 2 + side_of
        return remote(x_ref, rows_v.at[slot], rows_send.at[of], rows_recv.at[slot], buddy)

    def forward(of):
        slot = of * 2 + side
        return remote(
            rows_v.at[slot], rows_v.at[slot], fwd_send.at[of], rows_recv.at[slot], buddy
        )

    own_copy = remote(x_ref, rows_v.at[me], fwd_send.at[plane], rows_recv.at[me], buddy)
    others(lambda to: rows_copy(to).start())
    own_copy.start()
    rows_v[me] = x_ref[...]
    for copy in in_copies:
        copy.wait()
    gain_own[...] = out_gain_ref[...].astype(jnp.float32)
    gain_copy = remote(gain_own, gain_far, small_send.at[0], small_recv.at[0], across)
    gain_copy.start()

    def pass_on(of):
        rows_arrival(of, side).wait_recv()
        forward(of).start()

    early = [3, 1, 2] if planes == 4 else None
    others(pass_on, early)

    named, weights = routes_ref[...], rw_ref[...]
    corner = lax.broadcasted_iota(jnp.int32, (near, near), 0) == lax.broadcasted_iota(
        jnp.int32, (near, near), 1
    )
    for expert in range(weight_v.shape[0]):
        line = jnp.sum(jnp.where(named == expert, weights, 0.0), axis=0, keepdims=True)
        column = jnp.sum(jnp.where(corner, line, 0.0), axis=1, keepdims=True)
        weight_v[expert] = jnp.broadcast_to(column, (near, 128))

    gain = in_gain_ref[...].astype(jnp.float32)
    group = 16 // near

    def build(at, carry=0):
        block = jnp.concatenate(
            [rows_v[at * group + i].astype(jnp.float32) for i in range(group)], axis=0
        )
        where = pl.ds(at * 16 if isinstance(at, int) else pl.multiple_of(at * 16, 16), 16)
        squares = jnp.sum(block * block, axis=1, keepdims=True)
        for at_half in range(half):
            sums_own[at_half, where, 2 * cut :] = jnp.broadcast_to(squares, (16, 128))
        lhs_v[where, :] = (block * gain).astype(jnp.bfloat16)
        return carry

    def wait_far(of):
        rows_arrival(of, 1 - side).wait_recv()

    wait_far(plane)
    if n // group == 2 and planes == 4:
        others(wait_far, [1])
        build(plane // 2)
        others(wait_far, [3, 2])
        build(1 - plane // 2)
    else:
        others(wait_far)
        looped(n // group, build)

    sums_copies = []
    for at in range(pieces):
        gate_copies[at].wait()
        place = slice(at % 2 * cut, (at % 2 + 1) * cut)
        sums_own[at // 2, :, place] = jnp.dot(
            lhs_v[...], gate_v[:, columns(at)], preferred_element_type=jnp.float32
        )
        if at % 2 == 1:
            to = at // 2
            copy = remote(
                sums_own.at[to], sums_far.at[to], sums_send.at[to], sums_recv.at[to], twin
            )
            copy.start()
            sums_copies.append(copy)

    for at in range(half):
        sums_copies[at].wait_recv()
        squares = sums_own[at, :, 2 * cut :][:, :1] + sums_far[at, :, 2 * cut :][:, :1]
        scale = lax.rsqrt(squares / model + EPS)
        a = (sums_own[at, :, :cut] + sums_far[at, :, :cut]) * scale
        b = (sums_own[at, :, cut : 2 * cut] + sums_far[at, :, cut : 2 * cut]) * scale
        hidden_v[:, at * cut : (at + 1) * cut] = (a / (1.0 + jnp.exp(-a)) * b).astype(
            jnp.bfloat16
        )
    for copy in down_copies:
        copy.wait()

    middle = planes // 2

    def half_copy(to):
        where = pl.ds(to * middle, middle)
        return remote(
            part_v.at[where], half_v.at[where], half_send.at[to], half_recv.at[to], buddy
        )

    def ret_copy(to):
        return remote(
            sum_v.at[to], ret_v.at[plane], ret_send.at[to], ret_recv.at[plane], {"ep": to * 2 + side}
        )

    def ret_arrival(of):
        return remote(
            sum_v.at[of], ret_v.at[of], ret_send.at[of], ret_recv.at[of], {"ep": of * 2 + side}
        )

    def keep(at, block, where):
        even, odd = block[:near], block[near:]
        own_v[at, :, where] = jnp.where(side == 0, even, odd)
        part_v[at, :, where] = jnp.where(side == 0, odd, even).astype(jnp.bfloat16)

    tile = 512 if width % 512 == 0 else 128
    for start in range(0, width, tile):
        where = slice(start, start + tile)
        term = jnp.dot(hidden_v[...], down_v[:, where], preferred_element_type=jnp.float32)
        if planes <= 8:
            for at in range(planes):
                keep(at, term[at * 2 * near : (at + 1) * 2 * near], where)
        else:
            y_v[:, where] = term
    if planes > 8:

        def split(at, carry):
            first = pl.multiple_of(at * 2 * near, 2 * near)
            keep(at, y_v[pl.ds(first, 2 * near), :], slice(0, width))
            return carry

        lax.fori_loop(0, planes, split, 0)
    here = plane // middle
    half_copy(1 - here).start()
    half_copy(here).start()

    def joined(to):
        return (own_v[to] + half_v[to].astype(jnp.float32)).astype(jnp.bfloat16)

    def send_sum(to):
        sum_v[to] = joined(to)
        ret_copy(to).start()

    half_copy(1 - here).wait_recv()
    if planes == 4:
        others(send_sum, [3, 2])
        half_copy(here).wait_recv()
        others(send_sum, [1])
    else:
        half_copy(here).wait_recv()
        others(send_sum)
    ret_v[plane] = joined(plane)

    def weighted(at):
        return weight_v[at // (share_count // 2)][:, :1] * ret_v[at].astype(jnp.float32)

    total = x_ref[...].astype(jnp.float32)
    if planes <= 8:
        terms = [total + weighted(plane)]

        def arrive(of):
            ret_arrival(of).wait_recv()
            terms.append(terms[-1] + weighted(of))

        others(arrive, early)
        total = terms[-1]
    else:
        others(lambda of: ret_arrival(of).wait_recv())
        total = looped(planes, lambda at, carry: carry + weighted(at), total)
    out = total.astype(jnp.bfloat16)
    lo_ref[...] = out
    residual = out.astype(jnp.float32)
    lo_copy = remote(lo_ref, lo_far, small_send.at[1], small_recv.at[1], across)
    lo_copy.start()
    tot_own[...] = jnp.broadcast_to(
        jnp.sum(residual * residual, axis=1, keepdims=True), tot_own.shape
    )
    tail = [
        remote(tot_own, tot_diag, small_send.at[3], small_recv.at[3], diagonal),
        remote(tot_own, tot_far, small_send.at[2], small_recv.at[2], across),
        lo_copy,
    ]
    for copy in tail[:2]:
        copy.start()

    def drain(to):
        rows_copy(to).wait_send()
        forward(to).wait_send()
        ret_copy(to).wait_send()

    others(drain)
    half_copy(0).wait_send()
    half_copy(1).wait_send()
    for copy in [gain_copy, own_copy] + sums_copies:
        copy.wait_send()
    gain_copy.wait_recv()
    for copy in tail:
        copy.wait_recv()
    final = lax.rsqrt((tot_far[:, :1] + tot_diag[:, :1]) / model + EPS)
    handed_ref[...] = (lo_far[...].astype(jnp.float32) * final * gain_far[...]).astype(
        jnp.bfloat16
    )
    for copy in tail:
        copy.wait_send()


def deliver(lo_ref, handed_ref, lo_out, handed_out, sems):
    copies = [
        pltpu.make_async_copy(lo_ref, lo_out, sems.at[0]),
        pltpu.make_async_copy(handed_ref, handed_out, sems.at[1]),
    ]
    for copy in copies:
        copy.start()
    for copy in copies:
        copy.wait()


def body(section_rows, routes, route_weights, in_gain, gate_up, down, out_gain):
    near, width = section_rows.shape[1:]
    hidden = down.shape[2]
    topk = routes.shape[2]
    span = gate_up.shape[3]
    n = lax.axis_size("ep")
    share_count = min(16, n // 4)
    rows = n * near
    cut = min(512, hidden)
    pieces = span // cut
    vmem = pl.BlockSpec(memory_space=pltpu.VMEM)
    hbm = pl.BlockSpec(memory_space=pl.ANY)
    f32, bf16 = jnp.float32, jnp.bfloat16
    dma = pltpu.SemaphoreType.DMA
    layer_out, handed = pl.pallas_call(
        lambda *refs: kernel(share_count, *refs),
        out_shape=[pltpu.VMEM((near, width), bf16)] * 2,
        in_specs=[hbm] * 7,
        out_specs=[vmem] * 2,
        scratch_shapes=[
            pltpu.VMEM((near, width), bf16),
            pltpu.VMEM((topk, near), jnp.int32),
            pltpu.VMEM((topk, near), f32),
            pltpu.VMEM((1, width), bf16),
            pltpu.VMEM((1, width), bf16),
            pltpu.VMEM((width, span), bf16),
            pltpu.VMEM((hidden, width), bf16),
            pltpu.VMEM((n, near, width), bf16),
            pltpu.VMEM((rows, width), bf16),
            pltpu.VMEM((pieces // 2, rows, 2 * cut + 128), f32),
            pltpu.VMEM((pieces // 2, rows, 2 * cut + 128), f32),
            pltpu.VMEM((rows, hidden), bf16),
            pltpu.VMEM((rows, width), f32),
            pltpu.VMEM((n // 2, near, width), f32),
            pltpu.VMEM((n // 2, near, width), bf16),
            pltpu.VMEM((n // 2, near, width), bf16),
            pltpu.VMEM((n // 2, near, width), bf16),
            pltpu.VMEM((n // 2, near, width), bf16),
            pltpu.VMEM((1, width), f32),
            pltpu.VMEM((1, width), f32),
            pltpu.VMEM((near, width), bf16),
            pltpu.VMEM((near, 128), f32),
            pltpu.VMEM((n // share_count, near, 128), f32),
            pltpu.VMEM((near, 128), f32),
            pltpu.VMEM((near, 128), f32),
            dma((5,)),
            dma((pieces,)),
            dma((pieces // 2,)),
            dma((n // 2,)),
            dma((n,)),
            dma((n // 2,)),
            dma((2,)),
            dma((2,)),
            dma((n // 2,)),
            dma((n // 2,)),
            dma((pieces // 2,)),
            dma((pieces // 2,)),
            dma((4,)),
            dma((4,)),
        ],
        compiler_params=pltpu.CompilerParams(
            collective_id=0, has_side_effects=True, vmem_limit_bytes=60 * 2**20
        ),
        name="routed_layer",
    )(section_rows[0], routes[0].T, route_weights[0].T, in_gain, out_gain, gate_up[0, 0], down[0, 0])
    layer_out, handed = pl.pallas_call(
        deliver,
        out_shape=[jax.ShapeDtypeStruct((near, width), bf16)] * 2,
        in_specs=[vmem] * 2,
        out_specs=[hbm] * 2,
        scratch_shapes=[dma((2,))],
        compiler_params=pltpu.CompilerParams(vmem_limit_bytes=2 * 2**20),
        name="deliver",
    )(layer_out, handed)
    return (layer_out[None], handed[None])


def solution(mesh):
    return jax.shard_map(
        body,
        mesh=mesh,
        in_specs=(
            P("section", "ep", "tp"),
            P("section", "ep", None),
            P("section", "ep", None),
            P("section", "tp"),
            P("section", "ep", "tp", None),
            P("section", "ep", None, "tp"),
            P("section", "tp"),
        ),
        out_specs=(P("section", "ep", "tp"), P("section", "ep", "tp")),
        check_vma=False,
    )
```

```python
import jax
import jax.numpy as jnp
from jax import lax
from jax.experimental import pallas as pl
from jax.experimental.pallas import tpu as pltpu
from jax.sharding import PartitionSpec as P

MESH = pl.DeviceIdType.MESH
EPS = 1e-06


def looped(count, step, carry=0):
    if count <= 8:
        for at in range(count):
            carry = step(at, carry)
        return carry
    return lax.fori_loop(0, count, step, carry)


def remote(src, dst, send, recv, target):
    return pltpu.make_async_remote_copy(
        src_ref=src,
        dst_ref=dst,
        send_sem=send,
        recv_sem=recv,
        device_id=target,
        device_id_type=MESH,
    )


def kernel(
    share_count,
    x_hbm,
    routes_hbm,
    rw_hbm,
    in_gain_hbm,
    out_gain_hbm,
    gate_hbm,
    down_hbm,
    lo_ref,
    handed_ref,
    x_ref,
    routes_ref,
    rw_ref,
    in_gain_ref,
    out_gain_ref,
    gate_v,
    down_v,
    rows_v,
    lhs_v,
    sums_own,
    sums_far,
    hidden_v,
    y_v,
    own_v,
    part_v,
    half_v,
    sum_v,
    ret_v,
    gain_own,
    gain_far,
    lo_far,
    tot_own,
    weight_v,
    tot_far,
    tot_diag,
    in_sem,
    gate_sem,
    down_sem,
    rows_send,
    rows_recv,
    fwd_send,
    half_send,
    half_recv,
    ret_send,
    ret_recv,
    sums_send,
    sums_recv,
    small_send,
    small_recv,
):
    n = rows_v.shape[0]
    planes = n // 2
    rows = lhs_v.shape[0]
    width = y_v.shape[1]
    near = x_ref.shape[0]
    hidden = down_v.shape[0]
    model = 2 * width
    section = lax.axis_index("section")
    me = lax.axis_index("ep")
    core = lax.axis_index("tp")
    plane, side = me // 2, me % 2
    buddy = {"ep": me + 1 - 2 * side}
    twin = {"tp": 1 - core}
    across = {"section": 1 - section}
    diagonal = {"section": 1 - section, "tp": 1 - core}

    def others(step, order=None):
        if planes > 8:

            def one(at, carry):
                step((plane + 1 + at) % planes)
                return carry

            lax.fori_loop(0, planes - 1, one, 0)
            return
        for offset in order or range(planes - 1, 0, -1):
            target, bit = plane, 1
            while bit < planes:
                if offset & bit:
                    target = target + bit * (1 - 2 * ((plane // bit) % 2))
                bit *= 2
            step(target)

    x_copy = pltpu.make_async_copy(x_hbm, x_ref, in_sem.at[0])
    in_copies = [
        pltpu.make_async_copy(routes_hbm, routes_ref, in_sem.at[1]),
        pltpu.make_async_copy(rw_hbm, rw_ref, in_sem.at[2]),
        pltpu.make_async_copy(in_gain_hbm, in_gain_ref, in_sem.at[3]),
        pltpu.make_async_copy(out_gain_hbm, out_gain_ref, in_sem.at[4]),
    ]
    x_copy.start()
    for copy in in_copies:
        copy.start()

    barrier = pltpu.get_barrier_semaphore()

    def greet(target):
        pl.semaphore_signal(barrier, inc=1, device_id=target, device_id_type=MESH)

    others(lambda to: greet({"ep": to * 2 + side}))
    for target in (buddy, twin, across, diagonal):
        greet(target)

    def fetches(source, target, sems):
        step = source.shape[0] // sems.shape[0]
        return [
            pltpu.make_async_copy(
                source.at[at * step : (at + 1) * step],
                target.at[at * step : (at + 1) * step],
                sems.at[at],
            )
            for at in range(sems.shape[0])
        ]

    gate_copies = fetches(gate_hbm, gate_v, gate_sem)
    down_copies = fetches(down_hbm, down_v, down_sem)
    for copy in gate_copies + down_copies:
        copy.start()
    x_copy.wait()
    pl.semaphore_wait(barrier, planes + 3)

    def rows_copy(to):
        return remote(
            x_ref, rows_v.at[me], rows_send.at[to], rows_recv.at[me], {"ep": to * 2 + side}
        )

    def rows_arrival(of, side_of):
        slot = of * 2 + side_of
        return remote(x_ref, rows_v.at[slot], rows_send.at[of], rows_recv.at[slot], buddy)

    def forward(of):
        slot = of * 2 + side
        return remote(
            rows_v.at[slot], rows_v.at[slot], fwd_send.at[of], rows_recv.at[slot], buddy
        )

    own_copy = remote(x_ref, rows_v.at[me], fwd_send.at[plane], rows_recv.at[me], buddy)
    others(lambda to: rows_copy(to).start())
    own_copy.start()
    rows_v[me] = x_ref[...]
    for copy in in_copies:
        copy.wait()
    gain_own[...] = out_gain_ref[...].astype(jnp.float32)
    gain_copy = remote(gain_own, gain_far, small_send.at[0], small_recv.at[0], across)
    gain_copy.start()

    def pass_on(of):
        rows_arrival(of, side).wait_recv()
        forward(of).start()

    early = [3, 1, 2] if planes == 4 else None
    others(pass_on, early)

    named, weights = routes_ref[...], rw_ref[...]
    corner = lax.broadcasted_iota(jnp.int32, (near, near), 0) == lax.broadcasted_iota(
        jnp.int32, (near, near), 1
    )
    for expert in range(weight_v.shape[0]):
        line = jnp.sum(jnp.where(named == expert, weights, 0.0), axis=0, keepdims=True)
        column = jnp.sum(jnp.where(corner, line, 0.0), axis=1, keepdims=True)
        weight_v[expert] = jnp.broadcast_to(column, (near, 128))

    gain = in_gain_ref[...].astype(jnp.float32)
    group = 16 // near

    def build(at, carry=0):
        block = jnp.concatenate(
            [rows_v[at * group + i].astype(jnp.float32) for i in range(group)], axis=0
        )
        where = pl.ds(at * 16 if isinstance(at, int) else pl.multiple_of(at * 16, 16), 16)
        squares = jnp.sum(block * block, axis=1, keepdims=True)
        for at_part in range(2):
            sums_own[at_part, where, hidden:] = jnp.broadcast_to(squares, (16, 128))
        lhs_v[where, :] = (block * gain).astype(jnp.bfloat16)
        return carry

    def wait_far(of):
        rows_arrival(of, 1 - side).wait_recv()

    wait_far(plane)
    if n // group == 2 and planes == 4:
        others(wait_far, [1])
        build(plane // 2)
        others(wait_far, [3, 2])
        build(1 - plane // 2)
    else:
        others(wait_far)
        looped(n // group, build)

    for copy in gate_copies:
        copy.wait()
    sums_copies = []
    for at in range(2):
        sums_own[at, :, :hidden] = jnp.dot(
            lhs_v[...],
            gate_v[:, at * hidden : (at + 1) * hidden],
            preferred_element_type=jnp.float32,
        )
        copy = remote(
            sums_own.at[at], sums_far.at[at], sums_send.at[at], sums_recv.at[at], twin
        )
        copy.start()
        sums_copies.append(copy)

    sums_copies[0].wait_recv()
    squares = sums_own[0, :, hidden:][:, :1] + sums_far[0, :, hidden:][:, :1]
    scale = lax.rsqrt(squares / model + EPS)
    sums_copies[1].wait_recv()
    cut = min(256, hidden)
    for start in range(0, hidden, cut):
        where = slice(start, start + cut)
        a = (sums_own[0, :, where] + sums_far[0, :, where]) * scale
        b = (sums_own[1, :, where] + sums_far[1, :, where]) * scale
        hidden_v[:, where] = (a / (1.0 + jnp.exp(-a)) * b).astype(jnp.bfloat16)
    for copy in down_copies:
        copy.wait()

    middle = planes // 2

    def half_copy(to):
        where = pl.ds(to * middle, middle)
        return remote(
            part_v.at[where], half_v.at[where], half_send.at[to], half_recv.at[to], buddy
        )

    def ret_copy(to):
        return remote(
            sum_v.at[to], ret_v.at[plane], ret_send.at[to], ret_recv.at[plane], {"ep": to * 2 + side}
        )

    def ret_arrival(of):
        return remote(
            sum_v.at[of], ret_v.at[of], ret_send.at[of], ret_recv.at[of], {"ep": of * 2 + side}
        )

    def keep(at, block, where):
        even, odd = block[:near], block[near:]
        own_v[at, :, where] = jnp.where(side == 0, even, odd)
        part_v[at, :, where] = jnp.where(side == 0, odd, even).astype(jnp.bfloat16)

    tile = 1024 if rows <= 64 else 512
    for start in range(0, width, tile):
        where = slice(start, min(start + tile, width))
        term = jnp.dot(hidden_v[...], down_v[:, where], preferred_element_type=jnp.float32)
        if planes <= 8:
            for at in range(planes):
                keep(at, term[at * 2 * near : (at + 1) * 2 * near], where)
        else:
            y_v[:, where] = term
    if planes > 8:

        def split(at, carry):
            first = pl.multiple_of(at * 2 * near, 2 * near)
            keep(at, y_v[pl.ds(first, 2 * near), :], slice(0, width))
            return carry

        lax.fori_loop(0, planes, split, 0)
    here = plane // middle
    half_copy(1 - here).start()
    half_copy(here).start()

    def joined(to):
        return (own_v[to] + half_v[to].astype(jnp.float32)).astype(jnp.bfloat16)

    def send_sum(to):
        sum_v[to] = joined(to)
        ret_copy(to).start()

    half_copy(1 - here).wait_recv()
    if planes == 4:
        others(send_sum, [3, 2])
        half_copy(here).wait_recv()
        others(send_sum, [1])
    else:
        half_copy(here).wait_recv()
        others(send_sum)
    ret_v[plane] = joined(plane)

    def weighted(at):
        return weight_v[at // (share_count // 2)][:, :1] * ret_v[at].astype(jnp.float32)

    total = x_ref[...].astype(jnp.float32)
    if planes <= 8:
        terms = [total + weighted(plane)]

        def arrive(of):
            ret_arrival(of).wait_recv()
            terms.append(terms[-1] + weighted(of))

        others(arrive, early)
        total = terms[-1]
    else:
        others(lambda of: ret_arrival(of).wait_recv())
        total = looped(planes, lambda at, carry: carry + weighted(at), total)
    out = total.astype(jnp.bfloat16)
    lo_ref[...] = out
    residual = out.astype(jnp.float32)
    lo_copy = remote(lo_ref, lo_far, small_send.at[1], small_recv.at[1], across)
    lo_copy.start()
    tot_own[...] = jnp.broadcast_to(
        jnp.sum(residual * residual, axis=1, keepdims=True), tot_own.shape
    )
    tail = [
        remote(tot_own, tot_diag, small_send.at[3], small_recv.at[3], diagonal),
        remote(tot_own, tot_far, small_send.at[2], small_recv.at[2], across),
        lo_copy,
    ]
    for copy in tail[:2]:
        copy.start()

    def drain(to):
        rows_copy(to).wait_send()
        forward(to).wait_send()
        ret_copy(to).wait_send()

    others(drain)
    half_copy(0).wait_send()
    half_copy(1).wait_send()
    for copy in [gain_copy, own_copy] + sums_copies:
        copy.wait_send()
    gain_copy.wait_recv()
    for copy in tail:
        copy.wait_recv()
    final = lax.rsqrt((tot_far[:, :1] + tot_diag[:, :1]) / model + EPS)
    handed_ref[...] = (lo_far[...].astype(jnp.float32) * final * gain_far[...]).astype(
        jnp.bfloat16
    )
    for copy in tail:
        copy.wait_send()


def deliver(lo_ref, handed_ref, lo_out, handed_out, sems):
    copies = [
        pltpu.make_async_copy(lo_ref, lo_out, sems.at[0]),
        pltpu.make_async_copy(handed_ref, handed_out, sems.at[1]),
    ]
    for copy in copies:
        copy.start()
    for copy in copies:
        copy.wait()


def body(section_rows, routes, route_weights, in_gain, gate_up, down, out_gain):
    near, width = section_rows.shape[1:]
    hidden = down.shape[2]
    topk = routes.shape[2]
    span = gate_up.shape[3]
    n = lax.axis_size("ep")
    share_count = min(16, n // 4)
    rows = n * near
    vmem = pl.BlockSpec(memory_space=pltpu.VMEM)
    hbm = pl.BlockSpec(memory_space=pl.ANY)
    f32, bf16 = jnp.float32, jnp.bfloat16
    dma = pltpu.SemaphoreType.DMA
    layer_out, handed = pl.pallas_call(
        lambda *refs: kernel(share_count, *refs),
        out_shape=[pltpu.VMEM((near, width), bf16)] * 2,
        in_specs=[hbm] * 7,
        out_specs=[vmem] * 2,
        scratch_shapes=[
            pltpu.VMEM((near, width), bf16),
            pltpu.VMEM((topk, near), jnp.int32),
            pltpu.VMEM((topk, near), f32),
            pltpu.VMEM((1, width), bf16),
            pltpu.VMEM((1, width), bf16),
            pltpu.VMEM((width, span), bf16),
            pltpu.VMEM((hidden, width), bf16),
            pltpu.VMEM((n, near, width), bf16),
            pltpu.VMEM((rows, width), bf16),
            pltpu.VMEM((2, rows, hidden + 128), f32),
            pltpu.VMEM((2, rows, hidden + 128), f32),
            pltpu.VMEM((rows, hidden), bf16),
            pltpu.VMEM((rows, width), f32),
            pltpu.VMEM((n // 2, near, width), f32),
            pltpu.VMEM((n // 2, near, width), bf16),
            pltpu.VMEM((n // 2, near, width), bf16),
            pltpu.VMEM((n // 2, near, width), bf16),
            pltpu.VMEM((n // 2, near, width), bf16),
            pltpu.VMEM((1, width), f32),
            pltpu.VMEM((1, width), f32),
            pltpu.VMEM((near, width), bf16),
            pltpu.VMEM((near, 128), f32),
            pltpu.VMEM((n // share_count, near, 128), f32),
            pltpu.VMEM((near, 128), f32),
            pltpu.VMEM((near, 128), f32),
            dma((5,)),
            dma((8,)),
            dma((4,)),
            dma((n // 2,)),
            dma((n,)),
            dma((n // 2,)),
            dma((2,)),
            dma((2,)),
            dma((n // 2,)),
            dma((n // 2,)),
            dma((2,)),
            dma((2,)),
            dma((4,)),
            dma((4,)),
        ],
        compiler_params=pltpu.CompilerParams(
            collective_id=0, has_side_effects=True, vmem_limit_bytes=60 * 2**20
        ),
        name="routed_layer",
    )(section_rows[0], routes[0].T, route_weights[0].T, in_gain, out_gain, gate_up[0, 0], down[0, 0])
    layer_out, handed = pl.pallas_call(
        deliver,
        out_shape=[jax.ShapeDtypeStruct((near, width), bf16)] * 2,
        in_specs=[vmem] * 2,
        out_specs=[hbm] * 2,
        scratch_shapes=[dma((2,))],
        compiler_params=pltpu.CompilerParams(vmem_limit_bytes=2 * 2**20),
        name="deliver",
    )(layer_out, handed)
    return (layer_out[None], handed[None])


def solution(mesh):
    return jax.shard_map(
        body,
        mesh=mesh,
        in_specs=(
            P("section", "ep", "tp"),
            P("section", "ep", None),
            P("section", "ep", None),
            P("section", "tp"),
            P("section", "ep", "tp", None),
            P("section", "ep", None, "tp"),
            P("section", "tp"),
        ),
        out_specs=(P("section", "ep", "tp"), P("section", "ep", "tp")),
        check_vma=False,
    )
```

```python
import jax
import jax.numpy as jnp
from jax import lax
from jax.experimental import pallas as pl
from jax.experimental.pallas import tpu as pltpu
from jax.sharding import PartitionSpec as P

MESH = pl.DeviceIdType.MESH
EPS = 1e-06


def looped(count, step, carry=0):
    if count <= 8:
        for at in range(count):
            carry = step(at, carry)
        return carry
    return lax.fori_loop(0, count, step, carry)


def product(left, right, columns):
    depth = right.shape[0]
    step = depth // 2 if depth % 512 == 0 else depth
    terms = [
        jnp.dot(
            left[:, at : at + step],
            right[at : at + step, columns],
            preferred_element_type=jnp.float32,
        )
        for at in range(0, depth, step)
    ]
    return sum(terms[1:], terms[0])


def remote(src, dst, send, recv, target):
    return pltpu.make_async_remote_copy(
        src_ref=src,
        dst_ref=dst,
        send_sem=send,
        recv_sem=recv,
        device_id=target,
        device_id_type=MESH,
    )


def kernel(
    share_count,
    x_hbm,
    routes_hbm,
    rw_hbm,
    in_gain_hbm,
    out_gain_hbm,
    gate_hbm,
    down_hbm,
    lo_ref,
    handed_ref,
    x_ref,
    routes_ref,
    rw_ref,
    in_gain_ref,
    out_gain_ref,
    gate_v,
    down_v,
    rows_v,
    lhs_v,
    sums_own,
    sums_far,
    hidden_v,
    y_v,
    own_v,
    part_v,
    half_v,
    sum_v,
    ret_v,
    gain_own,
    gain_far,
    lo_far,
    tot_own,
    weight_v,
    tot_far,
    tot_diag,
    in_sem,
    gate_sem,
    down_sem,
    rows_send,
    rows_recv,
    fwd_send,
    half_send,
    half_recv,
    ret_send,
    ret_recv,
    sums_send,
    sums_recv,
    small_send,
    small_recv,
):
    n = rows_v.shape[0]
    planes = n // 2
    rows = lhs_v.shape[0]
    width = y_v.shape[1]
    near = x_ref.shape[0]
    hidden = down_v.shape[0]
    model = 2 * width
    section = lax.axis_index("section")
    me = lax.axis_index("ep")
    core = lax.axis_index("tp")
    plane, side = me // 2, me % 2
    buddy = {"ep": me + 1 - 2 * side}
    twin = {"tp": 1 - core}
    across = {"section": 1 - section}
    diagonal = {"section": 1 - section, "tp": 1 - core}

    def others(step, order=None):
        if planes > 8:

            def one(at, carry):
                step((plane + 1 + at) % planes)
                return carry

            lax.fori_loop(0, planes - 1, one, 0)
            return
        for offset in order or range(planes - 1, 0, -1):
            target, bit = plane, 1
            while bit < planes:
                if offset & bit:
                    target = target + bit * (1 - 2 * ((plane // bit) % 2))
                bit *= 2
            step(target)

    x_copy = pltpu.make_async_copy(x_hbm, x_ref, in_sem.at[0])
    in_copies = [
        pltpu.make_async_copy(routes_hbm, routes_ref, in_sem.at[1]),
        pltpu.make_async_copy(rw_hbm, rw_ref, in_sem.at[2]),
        pltpu.make_async_copy(in_gain_hbm, in_gain_ref, in_sem.at[3]),
        pltpu.make_async_copy(out_gain_hbm, out_gain_ref, in_sem.at[4]),
    ]
    x_copy.start()
    for copy in in_copies:
        copy.start()

    barrier = pltpu.get_barrier_semaphore()

    def greet(target):
        pl.semaphore_signal(barrier, inc=1, device_id=target, device_id_type=MESH)

    others(lambda to: greet({"ep": to * 2 + side}))
    for target in (buddy, twin, across, diagonal):
        greet(target)

    def fetches(source, target, sems):
        step = source.shape[0] // sems.shape[0]
        return [
            pltpu.make_async_copy(
                source.at[at * step : (at + 1) * step],
                target.at[at * step : (at + 1) * step],
                sems.at[at],
            )
            for at in range(sems.shape[0])
        ]

    gate_copies = fetches(gate_hbm, gate_v, gate_sem)
    down_copies = fetches(down_hbm, down_v, down_sem)
    for copy in gate_copies + down_copies:
        copy.start()
    x_copy.wait()
    pl.semaphore_wait(barrier, planes + 3)

    def rows_copy(to):
        return remote(
            x_ref, rows_v.at[me], rows_send.at[to], rows_recv.at[me], {"ep": to * 2 + side}
        )

    def rows_arrival(of, side_of):
        slot = of * 2 + side_of
        return remote(x_ref, rows_v.at[slot], rows_send.at[of], rows_recv.at[slot], buddy)

    def forward(of):
        slot = of * 2 + side
        return remote(
            rows_v.at[slot], rows_v.at[slot], fwd_send.at[of], rows_recv.at[slot], buddy
        )

    own_copy = remote(x_ref, rows_v.at[me], fwd_send.at[plane], rows_recv.at[me], buddy)
    others(lambda to: rows_copy(to).start())
    own_copy.start()
    rows_v[me] = x_ref[...]
    for copy in in_copies:
        copy.wait()
    gain_own[...] = out_gain_ref[...].astype(jnp.float32)
    gain_copy = remote(gain_own, gain_far, small_send.at[0], small_recv.at[0], across)
    gain_copy.start()

    def pass_on(of):
        rows_arrival(of, side).wait_recv()
        forward(of).start()

    early = [3, 1, 2] if planes == 4 else None
    others(pass_on, early)

    named, weights = routes_ref[...], rw_ref[...]
    corner = lax.broadcasted_iota(jnp.int32, (near, near), 0) == lax.broadcasted_iota(
        jnp.int32, (near, near), 1
    )
    for expert in range(weight_v.shape[0]):
        line = jnp.sum(jnp.where(named == expert, weights, 0.0), axis=0, keepdims=True)
        column = jnp.sum(jnp.where(corner, line, 0.0), axis=1, keepdims=True)
        weight_v[expert] = jnp.broadcast_to(column, (near, 128))

    gain = in_gain_ref[...].astype(jnp.float32)
    group = 16 // near

    def build(at, carry=0):
        block = jnp.concatenate(
            [rows_v[at * group + i].astype(jnp.float32) for i in range(group)], axis=0
        )
        where = pl.ds(at * 16 if isinstance(at, int) else pl.multiple_of(at * 16, 16), 16)
        squares = jnp.sum(block * block, axis=1, keepdims=True)
        for at_part in range(2):
            sums_own[at_part, where, hidden:] = jnp.broadcast_to(squares, (16, 128))
        lhs_v[where, :] = (block * gain).astype(jnp.bfloat16)
        return carry

    def wait_far(of):
        rows_arrival(of, 1 - side).wait_recv()

    wait_far(plane)
    if n // group == 2 and planes == 4:
        others(wait_far, [1])
        build(plane // 2)
        others(wait_far, [3, 2])
        build(1 - plane // 2)
    else:
        others(wait_far)
        looped(n // group, build)

    for copy in gate_copies:
        copy.wait()
    sums_copies = []
    for at in range(2):
        sums_own[at, :, :hidden] = product(lhs_v, gate_v, slice(at * hidden, (at + 1) * hidden))
        copy = remote(
            sums_own.at[at], sums_far.at[at], sums_send.at[at], sums_recv.at[at], twin
        )
        copy.start()
        sums_copies.append(copy)

    sums_copies[0].wait_recv()
    squares = sums_own[0, :, hidden:][:, :1] + sums_far[0, :, hidden:][:, :1]
    scale = lax.rsqrt(squares / model + EPS)
    sums_copies[1].wait_recv()
    cut = min(256, hidden)
    for start in range(0, hidden, cut):
        where = slice(start, start + cut)
        a = (sums_own[0, :, where] + sums_far[0, :, where]) * scale
        b = (sums_own[1, :, where] + sums_far[1, :, where]) * scale
        hidden_v[:, where] = (a / (1.0 + jnp.exp(-a)) * b).astype(jnp.bfloat16)
    for copy in down_copies:
        copy.wait()

    middle = planes // 2

    def half_copy(to):
        where = pl.ds(to * middle, middle)
        return remote(
            part_v.at[where], half_v.at[where], half_send.at[to], half_recv.at[to], buddy
        )

    def ret_copy(to):
        return remote(
            sum_v.at[to], ret_v.at[plane], ret_send.at[to], ret_recv.at[plane], {"ep": to * 2 + side}
        )

    def ret_arrival(of):
        return remote(
            sum_v.at[of], ret_v.at[of], ret_send.at[of], ret_recv.at[of], {"ep": of * 2 + side}
        )

    def keep(at, block, where):
        even, odd = block[:near], block[near:]
        own_v[at, :, where] = jnp.where(side == 0, even, odd)
        part_v[at, :, where] = jnp.where(side == 0, odd, even).astype(jnp.bfloat16)

    tile = 1024 if rows <= 64 else 512
    for start in range(0, width, tile):
        where = slice(start, min(start + tile, width))
        term = product(hidden_v, down_v, where)
        if planes <= 8:
            for at in range(planes):
                keep(at, term[at * 2 * near : (at + 1) * 2 * near], where)
        else:
            y_v[:, where] = term
    if planes > 8:

        def split(at, carry):
            first = pl.multiple_of(at * 2 * near, 2 * near)
            keep(at, y_v[pl.ds(first, 2 * near), :], slice(0, width))
            return carry

        lax.fori_loop(0, planes, split, 0)
    here = plane // middle
    half_copy(1 - here).start()
    half_copy(here).start()

    def joined(to):
        return (own_v[to] + half_v[to].astype(jnp.float32)).astype(jnp.bfloat16)

    def send_sum(to):
        sum_v[to] = joined(to)
        ret_copy(to).start()

    half_copy(1 - here).wait_recv()
    if planes == 4:
        others(send_sum, [3, 2])
        half_copy(here).wait_recv()
        others(send_sum, [1])
    else:
        half_copy(here).wait_recv()
        others(send_sum)
    ret_v[plane] = joined(plane)

    def weighted(at):
        return weight_v[at // (share_count // 2)][:, :1] * ret_v[at].astype(jnp.float32)

    total = x_ref[...].astype(jnp.float32)
    if planes <= 8:
        terms = [total + weighted(plane)]

        def arrive(of):
            ret_arrival(of).wait_recv()
            terms.append(terms[-1] + weighted(of))

        others(arrive, early)
        total = terms[-1]
    else:
        others(lambda of: ret_arrival(of).wait_recv())
        total = looped(planes, lambda at, carry: carry + weighted(at), total)
    out = total.astype(jnp.bfloat16)
    lo_ref[...] = out
    residual = out.astype(jnp.float32)
    lo_copy = remote(lo_ref, lo_far, small_send.at[1], small_recv.at[1], across)
    lo_copy.start()
    tot_own[...] = jnp.broadcast_to(
        jnp.sum(residual * residual, axis=1, keepdims=True), tot_own.shape
    )
    tail = [
        remote(tot_own, tot_diag, small_send.at[3], small_recv.at[3], diagonal),
        remote(tot_own, tot_far, small_send.at[2], small_recv.at[2], across),
        lo_copy,
    ]
    for copy in tail[:2]:
        copy.start()

    def drain(to):
        rows_copy(to).wait_send()
        forward(to).wait_send()
        ret_copy(to).wait_send()

    others(drain)
    half_copy(0).wait_send()
    half_copy(1).wait_send()
    for copy in [gain_copy, own_copy] + sums_copies:
        copy.wait_send()
    gain_copy.wait_recv()
    for copy in tail:
        copy.wait_recv()
    final = lax.rsqrt((tot_far[:, :1] + tot_diag[:, :1]) / model + EPS)
    handed_ref[...] = (lo_far[...].astype(jnp.float32) * final * gain_far[...]).astype(
        jnp.bfloat16
    )
    for copy in tail:
        copy.wait_send()


def deliver(lo_ref, handed_ref, lo_out, handed_out, sems):
    copies = [
        pltpu.make_async_copy(lo_ref, lo_out, sems.at[0]),
        pltpu.make_async_copy(handed_ref, handed_out, sems.at[1]),
    ]
    for copy in copies:
        copy.start()
    for copy in copies:
        copy.wait()


def body(section_rows, routes, route_weights, in_gain, gate_up, down, out_gain):
    near, width = section_rows.shape[1:]
    hidden = down.shape[2]
    topk = routes.shape[2]
    span = gate_up.shape[3]
    n = lax.axis_size("ep")
    share_count = min(16, n // 4)
    rows = n * near
    vmem = pl.BlockSpec(memory_space=pltpu.VMEM)
    hbm = pl.BlockSpec(memory_space=pl.ANY)
    f32, bf16 = jnp.float32, jnp.bfloat16
    dma = pltpu.SemaphoreType.DMA
    layer_out, handed = pl.pallas_call(
        lambda *refs: kernel(share_count, *refs),
        out_shape=[pltpu.VMEM((near, width), bf16)] * 2,
        in_specs=[hbm] * 7,
        out_specs=[vmem] * 2,
        scratch_shapes=[
            pltpu.VMEM((near, width), bf16),
            pltpu.VMEM((topk, near), jnp.int32),
            pltpu.VMEM((topk, near), f32),
            pltpu.VMEM((1, width), bf16),
            pltpu.VMEM((1, width), bf16),
            pltpu.VMEM((width, span), bf16),
            pltpu.VMEM((hidden, width), bf16),
            pltpu.VMEM((n, near, width), bf16),
            pltpu.VMEM((rows, width), bf16),
            pltpu.VMEM((2, rows, hidden + 128), f32),
            pltpu.VMEM((2, rows, hidden + 128), f32),
            pltpu.VMEM((rows, hidden), bf16),
            pltpu.VMEM((rows, width), f32),
            pltpu.VMEM((n // 2, near, width), f32),
            pltpu.VMEM((n // 2, near, width), bf16),
            pltpu.VMEM((n // 2, near, width), bf16),
            pltpu.VMEM((n // 2, near, width), bf16),
            pltpu.VMEM((n // 2, near, width), bf16),
            pltpu.VMEM((1, width), f32),
            pltpu.VMEM((1, width), f32),
            pltpu.VMEM((near, width), bf16),
            pltpu.VMEM((near, 128), f32),
            pltpu.VMEM((n // share_count, near, 128), f32),
            pltpu.VMEM((near, 128), f32),
            pltpu.VMEM((near, 128), f32),
            dma((5,)),
            dma((8,)),
            dma((4,)),
            dma((n // 2,)),
            dma((n,)),
            dma((n // 2,)),
            dma((2,)),
            dma((2,)),
            dma((n // 2,)),
            dma((n // 2,)),
            dma((2,)),
            dma((2,)),
            dma((4,)),
            dma((4,)),
        ],
        compiler_params=pltpu.CompilerParams(
            collective_id=0, has_side_effects=True, vmem_limit_bytes=60 * 2**20
        ),
        name="routed_layer",
    )(section_rows[0], routes[0].T, route_weights[0].T, in_gain, out_gain, gate_up[0, 0], down[0, 0])
    layer_out, handed = pl.pallas_call(
        deliver,
        out_shape=[jax.ShapeDtypeStruct((near, width), bf16)] * 2,
        in_specs=[vmem] * 2,
        out_specs=[hbm] * 2,
        scratch_shapes=[dma((2,))],
        compiler_params=pltpu.CompilerParams(vmem_limit_bytes=2 * 2**20),
        name="deliver",
    )(layer_out, handed)
    return (layer_out[None], handed[None])


def solution(mesh):
    return jax.shard_map(
        body,
        mesh=mesh,
        in_specs=(
            P("section", "ep", "tp"),
            P("section", "ep", None),
            P("section", "ep", None),
            P("section", "tp"),
            P("section", "ep", "tp", None),
            P("section", "ep", None, "tp"),
            P("section", "tp"),
        ),
        out_specs=(P("section", "ep", "tp"), P("section", "ep", "tp")),
        check_vma=False,
    )
```
